128 devices in a mesh: req: 8 (over x, core), exp: 16 (over y, z).
Axes of the slice: x: 4, y: 4, z: 4, core: 2. Of those that a mesh axis runs over, the one named last changes fastest.
Arguments:
- tokens: bfloat16 [8320, 2048], P('req'), may hold values from -6 to 6
- attn_gain: bfloat16 [2048], replicated, may hold values from 0.099609375 to 1.8984375
- wq_nope: bfloat16 [2048, 2048], P(None, 'exp'), may hold values from -0.125 to 0.125
- wq_rope: bfloat16 [2048, 1024], P(None, 'exp'), may hold values from -0.125 to 0.125
- w_latent: bfloat16 [2048, 512], replicated, may hold values from -0.125 to 0.125
- w_krope: bfloat16 [2048, 64], replicated, may hold values from -0.125 to 0.125
- latent_gain: bfloat16 [512], replicated, may hold values from 0.099609375 to 1.8984375
- w_uk: bfloat16 [512, 2048], P(None, 'exp'), may hold values from -0.25 to 0.25
- w_uv: bfloat16 [512, 2048], P(None, 'exp'), may hold values from -0.25 to 0.25
- w_out: bfloat16 [2048, 2048], P('exp'), may hold values from -0.125 to 0.125
- moe_gain: bfloat16 [2048], replicated, may hold values from 0.099609375 to 1.8984375
- w_router: bfloat16 [2048, 64], replicated, may hold values from -0.125 to 0.125
- w_gate: bfloat16 [128, 2048, 704], P(('req', 'exp')), may hold values from -0.125 to 0.125
- w_up: bfloat16 [128, 2048, 704], P(('req', 'exp')), may hold values from -0.125 to 0.125
- w_down: bfloat16 [128, 704, 2048], P(('req', 'exp')), may hold values from -0.15625 to 0.15625
- routes: int32 [8320, 6], P(('req', 'exp')), may hold values from 0 to 63, all different within a row; in each aligned block of 65 rows (0 to 64, 65 to 129, ...) at most 10 rows name the same one
- cache_latent: bfloat16 [128, 16, 32, 512], P('req', 'exp'), may hold values from -300 to 300
- cache_rope: bfloat16 [128, 16, 2048], P('req', 'exp'), may hold values from -6 to 6
- mig_dest: int32 [128], P('req'), may hold values from 0 to 7, as said below
- page_table: int32 [128, 16], P('req'), may hold values from 0 to 15, each once within a row
- cache_len: int32 [128], P('req'), may hold values from 1 to 512
- span_slot: int32 [8], P('req'), may hold values from 0 to 15
Outputs:
- mixed: bfloat16 [8320, 2048], P(('req', 'exp'))
The draws below stay inside these ranges and needn't reach their ends.
Inputs may be any that keep to these rules, and one draw needn't show every extreme that they name: `routes`: among the rows of one device, no expert is named by more than 10 rows, a bound that some block reaches. `mig_dest`: among the 16 slots of each group, exactly 2 go to each group, itself included.
All inputs are finite; a program needn't handle non-finite values.
Results may differ from the reference program's by a relative error of at most 0.019.
The reference program's roundings to bfloat16 on the way count: a program that leaves them out, or rounds other values in their place, can miss the bound.
Values may be sent and summed in bfloat16 or wider, within the bound.
No kernel may reach another device: no remote copies, remote signals or barrier semaphores. Data moves between devices by JAX's collectives and lax.ppermute only.
A program may use at most 128 MiB of HBM per device.

```python
import math
import jax
import jax.numpy as jnp
import numpy as np
from jax import lax

D = 2048
H = 16
DN = 128
DR = 64
DV = 128
R = 512
E = 64
FF = 1408
TOP = 6
PAGE = 32
SPAN = 1024
MOVE = 2
SPANS_GRP = 1
REQ_GRP = 16
NREQ = 128
MAXP = 16
CACHE = 512
ROWS_DEV = 65
ROWS = 8320
NSPAN = 8
FFH = 704
CAP = 10
N_REQ = 8
N_EXP = 16


def draw_cache_latent(key, part):
    normals = jax.random.normal(key, (NREQ, MAXP, PAGE, R), jnp.float32)
    return jnp.clip(normals, -6.0, 6.0).astype(jnp.bfloat16)


def draw_mig_dest(key, part):
    targets = jnp.tile(jnp.arange(N_REQ, dtype=jnp.int32), MOVE)
    group_keys = jax.random.split(key, N_REQ)
    return jax.vmap(lambda one_key: jax.random.permutation(one_key, targets))(group_keys).reshape(-1)


def touch_ends(array, rng, low, largest):
    index_at = [jax.random.randint(jax.random.fold_in(rng, axis), (), 0, length) for axis, length in enumerate(array.shape)]
    longest = array.shape.index(max(array.shape))
    neighbour = index_at[:longest] + [(index_at[longest] + 1) % array.shape[longest]] + index_at[longest + 1:]
    return array.at[tuple(index_at)].set(low).at[tuple(neighbour)].set(largest)


def level_of(rng, extent, pieces, smallest, high):
    gain, own = 1.0, jax.random.fold_in(rng, 6)
    for dim, parts in pieces:
        draws = jnp.exp(jax.random.uniform(jax.random.fold_in(own, dim), (parts,), jnp.float32, smallest / len(pieces), high / len(pieces)))
        gain = gain * jnp.repeat(draws, extent[dim] // parts).reshape([-1 if axis == dim else 1 for axis in range(len(extent))])
    return gain


def shared_out(rng, own, number, rows, number_of, top, reach, skew):
    ranking = jax.random.permutation(rng, number_of)
    crowded, usual = load_shares(number_of, rows * top, reach, skew, True), load_shares(number_of, rows * top, reach, skew, False)
    places = jnp.arange(number_of)

    def named(tallies, turn):
        used = int((tallies > 0).sum())
        fixed = max(1, used // 4)
        passed = fixed + (places - fixed + turn * (used - fixed)) % max(1, number_of - fixed)
        return jnp.zeros((number_of,), jnp.int32).at[ranking[jnp.where(places < fixed, places, passed)]].set(jnp.asarray(tallies, jnp.int32))

    tallies = jnp.where(number % 4 == 0, named(crowded, number // 4), named(usual, number - number // 4 - 1))
    mixed = jax.random.permutation(jax.random.fold_in(own, 3), number_of)
    donor, sink = mixed[0:number_of // 2 * 2:2], mixed[1:number_of // 2 * 2:2]
    room = jnp.minimum(tallies[donor] - 1, reach - tallies[sink]) // 2
    room = jnp.where((donor == ranking[0]) | (sink == ranking[0]) | (tallies[sink] == 0), 0, jnp.maximum(room, 0))
    passed = jax.random.randint(jax.random.fold_in(own, 4), (number_of // 2,), 0, 1 << 20) % (room + 1)
    tallies = tallies.at[donor].add(-passed).at[sink].add(passed)
    items = jnp.searchsorted(jnp.cumsum(tallies), jnp.arange(rows * top), side="right").astype(jnp.int32)
    listing = items.reshape(top, rows).T
    listing = listing[jax.random.permutation(jax.random.fold_in(own, 1), rows)]
    turn = jax.random.randint(jax.random.fold_in(own, 2), (rows, 1), 0, top)
    return jnp.take_along_axis(listing, (jnp.arange(top)[None, :] + turn) % top, axis=1)


def load_shares(amount, total, limit, lean, full):
    loads = [(1 << 20) // math.isqrt(rank ** lean) + 1 for rank in range(1, amount + 1)]
    largest = limit if full else min(limit, max(-(-total // amount), total * loads[0] // sum(loads)))
    least = 1 if total - largest >= amount - 1 else 0
    given, spare = [largest] + [least] * (amount - 1), total - largest - least * (amount - 1)
    while spare > 0:
        candidates = [i for i in range(1, amount) if given[i] < largest] or [i for i in range(1, amount) if given[i] < limit]
        mass, remaining = sum([loads[i] for i in candidates]), spare
        for i in candidates:
            addition = min(limit - given[i], max(1, remaining * loads[i] // mass), spare)
            given[i] = given[i] + addition
            spare = spare - addition
    return np.array(given)


def normal_values(own_key, shape, scale, bound, shards=(), kind=jnp.bfloat16):
    result = scale * jax.random.normal(own_key, shape, jnp.float32)
    if shards:
        result = result * level_of(own_key, shape, shards, -0.22, 0.18)
    return jnp.clip(result, -bound, bound).astype(kind)


def setup_inputs(seed: int = 0) -> dict:
    arg_keys = jax.random.split(jax.random.key(seed), 23)
    tokens = normal_values(arg_keys[0], (ROWS, D), 1.0, 6.0, ((0, 8),))
    attn_gain = jnp.clip(1.0 + 0.18 * jax.random.normal(arg_keys[1], (D,), jnp.float32), 0.099609375, 1.8984375).astype(jnp.bfloat16)
    wq_nope = normal_values(arg_keys[2], (D, H * DN), D ** -0.5, 0.125, ((1, 16),))
    wq_rope = normal_values(arg_keys[3], (D, H * DR), D ** -0.5, 0.125, ((1, 16),))
    w_latent = normal_values(arg_keys[4], (D, R), D ** -0.5, 0.125)
    w_krope = normal_values(arg_keys[5], (D, DR), D ** -0.5, 0.125)
    latent_gain = jnp.clip(1.0 + 0.18 * jax.random.normal(arg_keys[6], (R,), jnp.float32), 0.099609375, 1.8984375).astype(jnp.bfloat16)
    w_uk = normal_values(arg_keys[7], (R, H * DN), R ** -0.5, 0.25, ((1, 16),))
    w_uv = normal_values(arg_keys[8], (R, H * DV), R ** -0.5, 0.25, ((1, 16),))
    w_out = normal_values(arg_keys[9], (H * DV, D), (H * DV) ** -0.5, 0.125, ((0, 16),))
    moe_gain = jnp.clip(1.0 + 0.18 * jax.random.normal(arg_keys[10], (D,), jnp.float32), 0.099609375, 1.8984375).astype(jnp.bfloat16)
    w_router = normal_values(arg_keys[11], (D, E), D ** -0.5, 0.125)
    w_gate = normal_values(arg_keys[12], (2 * E, D, FFH), D ** -0.5, 0.125, ((0, 128),))
    w_up = normal_values(arg_keys[13], (2 * E, D, FFH), D ** -0.5, 0.125, ((0, 128),))
    w_down = normal_values(arg_keys[14], (2 * E, FFH, D), FF ** -0.5, 0.15625, ((0, 128),))
    routes_keys = jax.random.split(jax.random.fold_in(arg_keys[15], 1), ROWS // ROWS_DEV)
    routes_turns = jax.random.permutation(jax.random.fold_in(arg_keys[15], 3), ROWS // ROWS_DEV)
    routes = jax.vmap(lambda own, number: shared_out(jax.random.fold_in(arg_keys[15], 2), own, number, ROWS_DEV, E, TOP, CAP, 2))(routes_keys, routes_turns).reshape((ROWS, TOP))
    cache_latent = draw_cache_latent(jax.random.fold_in(arg_keys[22], 71), 0)
    cache_rope = normal_values(arg_keys[17], (NREQ, MAXP, PAGE * DR), 1.0, 6.0, ((0, 8), (1, 16)))
    mig_dest = draw_mig_dest(jax.random.fold_in(arg_keys[22], 71), 0)
    page_table = jax.vmap(lambda own: jax.random.permutation(own, MAXP))(jax.random.split(arg_keys[19], NREQ)).reshape((NREQ, MAXP)).astype(jnp.int32)
    cache_len = touch_ends(jax.random.randint(arg_keys[20], (NREQ,), 1, CACHE + 1), jax.random.fold_in(arg_keys[20], 1), 1, CACHE).astype(jnp.int32)
    span_slot = touch_ends(jax.random.randint(arg_keys[21], (NSPAN,), 0, REQ_GRP), jax.random.fold_in(arg_keys[21], 1), 0, REQ_GRP - 1).astype(jnp.int32)
    return dict(tokens=tokens, attn_gain=attn_gain, wq_nope=wq_nope, wq_rope=wq_rope, w_latent=w_latent, w_krope=w_krope, latent_gain=latent_gain, w_uk=w_uk, w_uv=w_uv, w_out=w_out, moe_gain=moe_gain, w_router=w_router, w_gate=w_gate, w_up=w_up, w_down=w_down, routes=routes, cache_latent=cache_latent, cache_rope=cache_rope, mig_dest=mig_dest, page_table=page_table, cache_len=cache_len, span_slot=span_slot)


theta_base = 50000.0
route_scale = 2.446
norm_eps = 1e-06

def rms_scale(values, gain_values):
    widened = values.astype(jnp.float32)
    mean_square = lax.optimization_barrier(jnp.mean(widened * widened, axis=-1, keepdims=True))
    return widened * lax.rsqrt(mean_square + norm_eps) * gain_values.astype(jnp.float32)

def rope_angles(positions, rope_width):
    exponent = jnp.arange(rope_width // 2, dtype=jnp.float32) * (2.0 / rope_width)
    frequency = jnp.exp(-exponent * math.log(theta_base))
    return positions.astype(jnp.float32)[:, None] * frequency[None, :]

def rotate(values, angles):
    half_width = values.shape[-1] // 2
    cosine = jnp.cos(angles)
    sine_part = jnp.sin(angles)
    first_half = values[..., :half_width]
    second_half = values[..., half_width:]
    return jnp.concatenate([first_half * cosine - second_half * sine_part, second_half * cosine + first_half * sine_part], axis=-1)

def group_positions(lengths, span_slots, span_width):
    starts = jnp.take(lengths, span_slots)
    span_positions = starts[:, None] + jnp.arange(span_width, dtype=jnp.int32)[None, :]
    return jnp.concatenate([span_positions.reshape(-1), lengths]).astype(jnp.int32)

def dot_transposed(left_side, right_side):
    return lax.dot_general(left_side, right_side, (((1,), (1,)), ((), ())), preferred_element_type=jnp.float32)

def soft_weights(scores, visible):
    masked = jnp.where(visible, scores, -jnp.inf)
    row_top = lax.optimization_barrier(jnp.max(masked, axis=-1, keepdims=True))
    raised = jnp.where(visible, jnp.exp(masked - row_top), 0.0)
    return (raised / lax.optimization_barrier(jnp.sum(raised, axis=-1, keepdims=True))).astype(jnp.bfloat16)

def attend_head(query_latent, query_rope, new_latent, new_rope, cache_keys, cache_rope_keys, lengths, span_slots, span_width, scale_factor):
    cache_size = cache_keys.shape[1]
    key_index = jnp.arange(cache_size + span_width, dtype=jnp.int32)
    row_index = jnp.arange(span_width, dtype=jnp.int32)
    results = []
    for span_idx in range(span_slots.shape[0]):
        row_start = span_idx * span_width
        request = span_slots[span_idx]
        keys_latent = jnp.concatenate([cache_keys[request], new_latent[row_start:row_start + span_width]], axis=0)
        keys_rope = jnp.concatenate([cache_rope_keys[request], new_rope[row_start:row_start + span_width]], axis=0)
        scores = (dot_transposed(query_latent[row_start:row_start + span_width], keys_latent) + dot_transposed(query_rope[row_start:row_start + span_width], keys_rope)) * scale_factor
        visible = jnp.where(key_index[None, :] < cache_size, key_index[None, :] < lengths[request], key_index[None, :] - cache_size <= row_index[:, None])
        weights = soft_weights(scores, visible)
        results.append(jnp.dot(weights, keys_latent, preferred_element_type=jnp.float32).astype(jnp.bfloat16))
    dec_start = span_slots.shape[0] * span_width
    dec_latent = query_latent[dec_start:].astype(jnp.float32)
    dec_rope = query_rope[dec_start:].astype(jnp.float32)
    own_latent = new_latent[dec_start:].astype(jnp.float32)
    own_rope = new_rope[dec_start:].astype(jnp.float32)
    cache_scores = (jnp.einsum('jr,jpr->jp', dec_latent, cache_keys.astype(jnp.float32)) + jnp.einsum('je,jpe->jp', dec_rope, cache_rope_keys.astype(jnp.float32))) * scale_factor
    self_scores = (lax.optimization_barrier(jnp.sum(dec_latent * own_latent, axis=1)) + lax.optimization_barrier(jnp.sum(dec_rope * own_rope, axis=1))) * scale_factor
    seen = jnp.arange(cache_size, dtype=jnp.int32)[None, :] < lengths[:, None]
    masked = jnp.where(seen, cache_scores, -jnp.inf)
    row_top = jnp.maximum(lax.optimization_barrier(jnp.max(masked, axis=1)), self_scores)
    cache_raised = jnp.where(seen, jnp.exp(masked - row_top[:, None]), 0.0)
    self_raised = jnp.exp(self_scores - row_top)
    totals = lax.optimization_barrier(jnp.sum(cache_raised, axis=1)) + self_raised
    cache_weights = (cache_raised / totals[:, None]).astype(jnp.bfloat16)
    self_weights = (self_raised / totals).astype(jnp.bfloat16)
    dec_out = jnp.einsum('jp,jpr->jr', cache_weights.astype(jnp.float32), cache_keys.astype(jnp.float32)) + self_weights.astype(jnp.float32)[:, None] * own_latent
    results.append(dec_out.astype(jnp.bfloat16))
    return jnp.concatenate(results, axis=0)

def reference(tokens, attn_gain, wq_nope, wq_rope, w_latent, w_krope, latent_gain, w_uk, w_uv, w_out, moe_gain, w_router, w_gate, w_up, w_down, routes, cache_latent, cache_rope, mig_dest, page_table, cache_len, span_slot):
    req_group = MOVE * N_REQ
    rows_group = SPANS_GRP * SPAN + req_group
    rows_device = rows_group // N_EXP
    heads_device = H // N_EXP
    device_count = N_REQ * N_EXP
    scale_factor = 1.0 / math.sqrt(DN + DR)
    total_requests = mig_dest.shape[0]
    new_order = jnp.argsort(mig_dest * total_requests + jnp.arange(total_requests, dtype=jnp.int32))
    moved_latent = cache_latent[new_order]
    moved_rope = cache_rope[new_order]
    resid_parts = []
    for group_idx in range(N_REQ):
        first_req = group_idx * req_group
        page_rows = page_table[first_req:first_req + req_group]
        latent_pages = jnp.take_along_axis(moved_latent[first_req:first_req + req_group], page_rows[:, :, None, None], axis=1)
        cache_keys = latent_pages.reshape(req_group, CACHE, R)
        rope_pages = jnp.take_along_axis(moved_rope[first_req:first_req + req_group], page_rows[:, :, None], axis=1)
        cache_rope_keys = rope_pages.reshape(req_group, CACHE, DR)
        lengths = cache_len[first_req:first_req + req_group]
        span_slots = span_slot[group_idx * SPANS_GRP:(group_idx + 1) * SPANS_GRP]
        group_tokens = tokens[group_idx * rows_group:(group_idx + 1) * rows_group]
        normed = rms_scale(group_tokens, attn_gain).astype(jnp.bfloat16)
        angles = rope_angles(group_positions(lengths, span_slots, SPAN), DR)
        query_nope = jnp.dot(normed, wq_nope, preferred_element_type=jnp.float32).astype(jnp.bfloat16)
        query_rope = rotate(jnp.dot(normed, wq_rope, preferred_element_type=jnp.float32).reshape(rows_group, H, DR), angles[:, None, :]).astype(jnp.bfloat16)
        new_latent = rms_scale(jnp.dot(normed, w_latent, preferred_element_type=jnp.float32), latent_gain).astype(jnp.bfloat16)
        new_rope = rotate(jnp.dot(normed, w_krope, preferred_element_type=jnp.float32), angles).astype(jnp.bfloat16)
        query_latent = jnp.einsum('thd,rhd->htr', query_nope.reshape(rows_group, H, DN).astype(jnp.float32), w_uk.reshape(R, H, DN).astype(jnp.float32)).astype(jnp.bfloat16)

        def one_head(head_items):
            return attend_head(head_items[0], head_items[1], new_latent, new_rope, cache_keys, cache_rope_keys, lengths, span_slots, SPAN, scale_factor)
        attended = lax.map(one_head, (query_latent, jnp.transpose(query_rope, (1, 0, 2))))
        head_out = jnp.einsum('htr,rhv->thv', attended.astype(jnp.float32), w_uv.reshape(R, H, DV).astype(jnp.float32)).astype(jnp.bfloat16).reshape(rows_group, H * DV)
        attn_total = jnp.zeros((rows_group, D), jnp.float32)
        for exp_idx in range(N_EXP):
            col_start = exp_idx * heads_device * DV
            col_end = col_start + heads_device * DV
            attn_part = jnp.dot(head_out[:, col_start:col_end], w_out[col_start:col_end], preferred_element_type=jnp.float32).astype(jnp.bfloat16)
            attn_part = lax.optimization_barrier(attn_part)
            attn_total = attn_total + attn_part.astype(jnp.float32)
        resid_parts.append((group_tokens.astype(jnp.float32) + attn_total).astype(jnp.bfloat16))
    resid = jnp.concatenate(resid_parts, axis=0)
    row_total = resid.shape[0]
    moe_in = rms_scale(resid, moe_gain).astype(jnp.bfloat16)
    scores = jax.nn.sigmoid(jnp.dot(moe_in, w_router, preferred_element_type=jnp.float32))
    picked = jnp.take_along_axis(scores, routes, axis=1)
    gate_w = route_scale * picked / lax.optimization_barrier(jnp.sum(picked, axis=1, keepdims=True))
    blocks = routes.reshape(device_count, rows_device * TOP)
    onehot = (blocks[:, :, None] == jnp.arange(E, dtype=jnp.int32)[None, None, :]).astype(jnp.int32)
    slot_rank = lax.optimization_barrier(jnp.sum((jnp.cumsum(onehot, axis=1) - 1) * onehot, axis=2))
    position = (jnp.arange(device_count, dtype=jnp.int32)[:, None] * CAP + slot_rank).reshape(-1).astype(jnp.int32)
    expert_ids = blocks.reshape(-1)
    token_ids = (jnp.arange(row_total * TOP, dtype=jnp.int32) // TOP).astype(jnp.int32)
    token_table = jnp.full((E, device_count * CAP), row_total, jnp.int32).at[expert_ids, position].set(token_ids)
    weight_table = jnp.zeros((E, device_count * CAP), jnp.float32).at[expert_ids, position].set(gate_w.reshape(-1))
    padded_in = jnp.concatenate([moe_in, jnp.zeros((1, D), jnp.bfloat16)], axis=0)

    def expert_step(running, step_items):
        token_idx, weight_col, gate_pair, up_pair, down_pair = step_items
        inputs = padded_in[token_idx]
        output = jnp.zeros((token_idx.shape[0], D), jnp.float32)
        for half_idx in range(2):
            hidden = (jax.nn.silu(jnp.dot(inputs, gate_pair[half_idx], preferred_element_type=jnp.float32)) * jnp.dot(inputs, up_pair[half_idx], preferred_element_type=jnp.float32)).astype(jnp.bfloat16)
            half_out = jnp.dot(hidden, down_pair[half_idx], preferred_element_type=jnp.float32).astype(jnp.bfloat16)
            half_out = lax.optimization_barrier(half_out)
            output = output + half_out.astype(jnp.float32)
        expert_out = lax.optimization_barrier(output.astype(jnp.bfloat16))
        running = running.at[token_idx].add(weight_col[:, None] * expert_out.astype(jnp.float32), mode='drop')
        return (running, None)
    moe_out = lax.scan(expert_step, jnp.zeros((row_total, D), jnp.float32), (token_table, weight_table, w_gate.reshape(E, 2, D, FFH), w_up.reshape(E, 2, D, FFH), w_down.reshape(E, 2, FFH, D)))[0]
    return (resid.astype(jnp.float32) + moe_out).astype(jnp.bfloat16)
```

```python
import functools
import math

import jax
import jax.numpy as jnp
from jax import lax
from jax.experimental import pallas as pl
from jax.experimental.pallas import tpu as pltpu
from jax.sharding import PartitionSpec as P

DN = 128
DR = 64
RANK = 512
KEY = RANK + DR
TOP = 6
SPAN = 1024
LANES = 128
F32 = jnp.float32
BF16 = jnp.bfloat16
MIB = 1 << 20

theta_base = 50000.0
route_scale = 2.446
norm_eps = 1e-06


def rms_scale(values, gain_values):
    widened = values.astype(F32)
    mean_square = jnp.mean(widened * widened, axis=-1, keepdims=True)
    return widened * lax.rsqrt(mean_square + norm_eps) * gain_values.astype(F32)


def rope_angles(positions, rope_width):
    exponent = jnp.arange(rope_width // 2, dtype=F32) * (2.0 / rope_width)
    frequency = jnp.exp(-exponent * math.log(theta_base))
    return positions.astype(F32)[:, None] * frequency[None, :]


def rotate(values, cosine, sine):
    half = values.shape[-1] // 2
    first, second = values[..., :half], values[..., half:]
    return jnp.concatenate(
        [first * cosine - second * sine, second * cosine + first * sine], axis=-1
    )


def dot(a, b):
    return jnp.dot(a, b, preferred_element_type=F32)


def dot_t(a, b):
    return lax.dot_general(a, b, (((1,), (1,)), ((), ())), preferred_element_type=F32)


def whole(shape):
    return pl.BlockSpec(shape, lambda *_: (0,) * len(shape))


def pack_kernel(table, rows_ref, out_ref, padded):
    experts, _, cap = out_ref.shape[:3]
    count = rows_ref.shape[0]
    padded[0:count] = rows_ref[...]
    padded[count] = jnp.zeros(padded.shape[1:], padded.dtype)
    first = pl.program_id(0) * experts

    def one(e, carry):
        for c in range(cap):
            row = padded[table[(first + e) * cap + c]]
            out_ref[e, 0, c] = row
            out_ref[e, 1, c] = row
        return carry

    lax.fori_loop(0, experts, one, 0)


def pack_rows(table, rows, experts, cap):
    count, blocks, lanes = rows.shape
    step = 8
    return pl.pallas_call(
        pack_kernel,
        grid_spec=pltpu.PrefetchScalarGridSpec(
            num_scalar_prefetch=1,
            grid=(experts // step,),
            in_specs=[pl.BlockSpec((count, blocks, lanes), lambda i, t: (0, 0, 0))],
            out_specs=pl.BlockSpec(
                (step, 2, cap, blocks, lanes), lambda i, t: (i, 0, 0, 0, 0)
            ),
            scratch_shapes=[pltpu.VMEM((count + 1, blocks, lanes), rows.dtype)],
        ),
        out_shape=jax.ShapeDtypeStruct((experts, 2, cap, blocks, lanes), rows.dtype),
        compiler_params=pltpu.CompilerParams(vmem_limit_bytes=32 * MIB),
    )(table, rows)


def combine_kernel(slots, gates, half_ref, resid_ref, out_ref):
    cap = half_ref.shape[1]

    def one(t, carry):
        total = resid_ref[t].astype(F32)
        mixed = jnp.zeros_like(total)
        for k in range(TOP):
            slot = slots[t * TOP + k]
            expert = slot // cap
            place = slot - expert * cap
            both = half_ref[2 * expert, place].astype(F32) + half_ref[
                2 * expert + 1, place
            ].astype(F32)
            mixed = mixed + gates[t * TOP + k] * both.astype(BF16).astype(F32)
        out_ref[t] = (total + mixed).astype(BF16)
        return carry

    lax.fori_loop(0, out_ref.shape[0], one, 0)


def combine_rows(slots, gates, halves, resid):
    return pl.pallas_call(
        combine_kernel,
        grid_spec=pltpu.PrefetchScalarGridSpec(
            num_scalar_prefetch=2,
            grid=(1,),
            in_specs=[
                pl.BlockSpec(halves.shape, lambda i, s, g: (0, 0, 0, 0)),
                pl.BlockSpec(resid.shape, lambda i, s, g: (0, 0, 0)),
            ],
            out_specs=pl.BlockSpec(resid.shape, lambda i, s, g: (0, 0, 0)),
        ),
        out_shape=jax.ShapeDtypeStruct(resid.shape, BF16),
        compiler_params=pltpu.CompilerParams(vmem_limit_bytes=32 * MIB),
    )(slots, gates, halves, resid)


def expert_kernel(x_ref, gate_ref, up_ref, down_ref, out_ref, wide, lhs):
    blocks = x_ref.shape[1]
    wide[...] = x_ref[...].astype(F32)
    for c in range(blocks):
        lhs[:, c * LANES : (c + 1) * LANES] = wide[:, c, :].astype(BF16)
    x = lhs[...]
    hidden_gate = dot(x, gate_ref[0])
    hidden_up = dot(x, up_ref[0])
    hidden = (hidden_gate / (1.0 + jnp.exp(-hidden_gate)) * hidden_up).astype(BF16)
    step = 4 * LANES
    for n in range(0, blocks * LANES, step):
        part = dot(hidden, down_ref[0, :, n : n + step]).astype(BF16).astype(F32)
        for c in range(step // LANES):
            wide[:, n // LANES + c, :] = part[:, c * LANES : (c + 1) * LANES]
    out_ref[...] = wide[...].astype(BF16)


def expert_rows(x, w_gate, w_up, w_down):
    rows, blocks, lanes = x.shape
    step = 320
    resident = functools.partial(pl.BlockSpec, pipeline_mode=pl.Buffered(1))
    return pl.pallas_call(
        expert_kernel,
        grid=(rows // step,),
        in_specs=[
            pl.BlockSpec((step, blocks, lanes), lambda i: (i, 0, 0)),
            resident(w_gate.shape, lambda i: (0, 0, 0)),
            resident(w_up.shape, lambda i: (0, 0, 0)),
            resident(w_down.shape, lambda i: (0, 0, 0)),
        ],
        out_specs=pl.BlockSpec((step, blocks, lanes), lambda i: (i, 0, 0)),
        out_shape=jax.ShapeDtypeStruct(x.shape, BF16),
        scratch_shapes=[
            pltpu.VMEM((step, blocks, lanes), F32),
            pltpu.VMEM((step, blocks * lanes), BF16),
        ],
        compiler_params=pltpu.CompilerParams(vmem_limit_bytes=48 * MIB),
    )(x, w_gate, w_up, w_down)


def softmax_rows(scores, visible):
    masked = jnp.where(visible, scores, -jnp.inf)
    row_top = jnp.max(masked, axis=-1, keepdims=True)
    raised = jnp.where(visible, jnp.exp(masked - row_top), 0.0)
    return (raised / jnp.sum(raised, axis=-1, keepdims=True)).astype(BF16)


def block_positions(page_row, page_size):
    pages = page_row.shape[0]
    ids = jnp.arange(pages, dtype=jnp.int32)
    logical = jnp.sum(
        jnp.where(page_row[:, None] == ids[None, :], ids[:, None], 0), axis=0
    )
    inside = jnp.arange(page_size, dtype=jnp.int32)
    return (logical[:, None] * page_size + inside[None, :]).reshape(-1)


def shards(
    tokens,
    attn_gain,
    wq_nope,
    wq_rope,
    w_latent,
    w_krope,
    latent_gain,
    w_uk,
    w_uv,
    w_out,
    moe_gain,
    w_router,
    w_gate,
    w_up,
    w_down,
    routes,
    cache_latent,
    cache_rope,
    mig_dest,
    page_table,
    cache_len,
    span_slot,
):
    req_count = lax.axis_size("req")
    exp_count = lax.axis_size("exp")
    device_count = req_count * exp_count
    own_exp = lax.axis_index("exp")
    req_group = mig_dest.shape[0]
    move_count = req_group // req_count
    page_size = cache_latent.shape[2]
    rows_group, width = tokens.shape
    rows_device = rows_group // exp_count
    blocks = width // LANES
    scale_factor = 1.0 / math.sqrt(DN + DR)

    w_out_all = lax.all_gather(w_out, "exp", axis=0, tiled=True)

    expert_count = w_router.shape[1]
    capacity = 2 * ((rows_device * TOP // expert_count + 5) // 2)
    expert_ids = jnp.arange(expert_count, dtype=jnp.int32)
    named = routes[:, :, None] == expert_ids[None, None, :]
    member = jnp.any(named, axis=1)
    row_ids = jnp.arange(rows_device, dtype=jnp.int32)
    before = (row_ids[None, :] < row_ids[:, None]).astype(BF16)
    rank = dot(before, member.astype(BF16)).astype(jnp.int32)
    slot_of = jnp.sum(
        jnp.where(named, rank[:, None, :] + expert_ids[None, None, :] * capacity, 0), axis=2
    )
    place_ids = jnp.arange(capacity, dtype=jnp.int32)
    filled = member[:, :, None] & (rank[:, :, None] == place_ids[None, None, :])
    table = rows_device + jnp.sum(
        jnp.where(filled, row_ids[:, None, None] - rows_device, 0), axis=0
    )

    slot_ids = jnp.arange(req_group, dtype=jnp.int32)
    earlier = (mig_dest[None, :] == mig_dest[:, None]) & (slot_ids[None, :] < slot_ids[:, None])
    placed = mig_dest * move_count + jnp.sum(earlier.astype(jnp.int32), axis=1)
    order = (placed[None, :] == slot_ids[:, None]).astype(BF16)
    pages = jnp.concatenate(
        [cache_latent[:, 0], cache_rope.reshape(req_group, page_size, DR)], axis=2
    )
    outgoing = jnp.einsum("os,sik->oik", order, pages, preferred_element_type=F32).astype(BF16)
    arrived = lax.all_to_all(
        outgoing.reshape(req_count, move_count * page_size, KEY),
        "req",
        split_axis=0,
        concat_axis=0,
        tiled=True,
    ).reshape(req_group, page_size, KEY)

    normed = rms_scale(tokens, attn_gain).astype(BF16)
    span_len = lax.dynamic_index_in_dim(cache_len, span_slot[0], 0, keepdims=False)
    positions = jnp.concatenate([span_len + jnp.arange(SPAN, dtype=jnp.int32), cache_len])
    angles = rope_angles(positions, DR)
    cosine, sine = jnp.cos(angles), jnp.sin(angles)
    query_nope = dot(normed, wq_nope).astype(BF16)
    query_rope = rotate(dot(normed, wq_rope), cosine, sine).astype(BF16)
    query = jnp.concatenate([dot_t(query_nope, w_uk).astype(BF16), query_rope], axis=1)
    new_keys = jnp.concatenate(
        [
            rms_scale(dot(normed, w_latent), latent_gain).astype(BF16),
            rotate(dot(normed, w_krope), cosine, sine).astype(BF16),
        ],
        axis=1,
    )

    span_page = lax.dynamic_index_in_dim(arrived, span_slot[0], 0)
    message = jnp.concatenate(
        [
            jnp.broadcast_to(span_page, arrived.shape),
            arrived,
            query[SPAN:, None, :],
            jnp.zeros((req_group, 7, KEY), BF16),
        ],
        axis=1,
    )
    message = lax.all_to_all(message, "exp", split_axis=0, concat_axis=0, tiled=True)
    span_cache = message[:, :page_size].reshape(-1, KEY)
    own_cache = message[:, page_size : 2 * page_size].reshape(-1, KEY)
    own_query = message[:, 2 * page_size]

    own_len = lax.dynamic_index_in_dim(cache_len, own_exp, 0, keepdims=False)
    own_pages = lax.dynamic_index_in_dim(page_table, own_exp, 0, keepdims=False)
    own_key = lax.dynamic_slice_in_dim(new_keys, SPAN + own_exp, 1, 0)
    own_seen = block_positions(own_pages, page_size) < own_len
    own_scores = dot_t(own_query, own_cache) * scale_factor
    self_score = (
        jnp.sum(own_query.astype(F32) * own_key.astype(F32), axis=1, keepdims=True) * scale_factor
    )
    own_masked = jnp.where(own_seen[None, :], own_scores, -jnp.inf)
    own_top = jnp.maximum(jnp.max(own_masked, axis=1, keepdims=True), self_score)
    own_raised = jnp.where(own_seen[None, :], jnp.exp(own_masked - own_top), 0.0)
    self_raised = jnp.exp(self_score - own_top)
    own_total = jnp.sum(own_raised, axis=1, keepdims=True) + self_raised
    own_out = (
        dot((own_raised / own_total).astype(BF16), own_cache[:, :RANK])
        + (self_raised / own_total).astype(BF16).astype(F32) * own_key[:, :RANK].astype(F32)
    ).astype(BF16)
    decode_out = lax.all_to_all(
        own_out[:, None, :], "exp", split_axis=0, concat_axis=0, tiled=True
    )[:, 0]

    span_table = lax.dynamic_index_in_dim(page_table, span_slot[0], 0, keepdims=False)
    span_seen = block_positions(span_table, page_size) < span_len
    key_ids = jnp.arange(SPAN, dtype=jnp.int32)
    keys = jnp.concatenate([span_cache, new_keys[:SPAN]], axis=0)
    visible = jnp.concatenate(
        [
            jnp.broadcast_to(span_seen[None, :], (SPAN, span_seen.shape[0])),
            key_ids[None, :] <= key_ids[:, None],
        ],
        axis=1,
    )
    weights = softmax_rows(dot_t(query[:SPAN], keys) * scale_factor, visible)
    span_out = dot(weights, keys[:, :RANK]).astype(BF16)
    attended = jnp.concatenate([span_out, decode_out], axis=0)
    head_out = dot(attended, w_uv).astype(BF16)

    heads_in = lax.all_to_all(
        head_out.reshape(exp_count, rows_device, DN),
        "exp",
        split_axis=0,
        concat_axis=0,
        tiled=True,
    )
    own_heads = jnp.transpose(heads_in, (1, 0, 2)).reshape(rows_device, width)
    own_tokens = lax.dynamic_slice_in_dim(tokens, own_exp * rows_device, rows_device, 0)
    resid = (own_tokens.astype(F32) + dot(own_heads, w_out_all)).astype(BF16)
    moe_in = rms_scale(resid, moe_gain).astype(BF16)
    scores = jax.nn.sigmoid(dot(moe_in, w_router))
    picked = jnp.sum(jnp.where(named, scores[:, None, :], 0.0), axis=2)
    gate_w = route_scale * picked / jnp.sum(picked, axis=1, keepdims=True)

    packed = pack_rows(
        table.reshape(-1),
        moe_in.reshape(rows_device, blocks, LANES),
        expert_count,
        capacity,
    )
    received = lax.all_to_all(
        packed.reshape(device_count, capacity * blocks, LANES),
        ("req", "exp"),
        split_axis=0,
        concat_axis=0,
        tiled=True,
    )
    computed = expert_rows(
        received.reshape(device_count * capacity, blocks, LANES), w_gate, w_up, w_down
    )
    returned = lax.all_to_all(
        computed.reshape(device_count, capacity * blocks, LANES),
        ("req", "exp"),
        split_axis=0,
        concat_axis=0,
        tiled=True,
    )
    mixed = combine_rows(
        slot_of.reshape(-1),
        gate_w.reshape(-1),
        returned.reshape(device_count, capacity, blocks, LANES),
        resid.reshape(rows_device, blocks, LANES),
    )
    return mixed.reshape(rows_device, width)


def solution(mesh):
    in_specs = (
        P("req", None),
        P(),
        P(None, "exp"),
        P(None, "exp"),
        P(),
        P(),
        P(),
        P(None, "exp"),
        P(None, "exp"),
        P("exp", None),
        P(),
        P(),
        P(("req", "exp"), None, None),
        P(("req", "exp"), None, None),
        P(("req", "exp"), None, None),
        P(("req", "exp"), None),
        P("req", "exp", None, None),
        P("req", "exp", None),
        P("req"),
        P("req", None),
        P("req"),
        P("req"),
    )
    out_specs = P(("req", "exp"), None)
    return jax.shard_map(shards, mesh=mesh, in_specs=in_specs, out_specs=out_specs, check_vma=False)
```

```python
import functools
import math

import jax
import jax.numpy as jnp
from jax import lax
from jax.experimental import pallas as pl
from jax.experimental.pallas import tpu as pltpu
from jax.sharding import PartitionSpec as P

DN = 128
DR = 64
RANK = 512
KEY = RANK + DR
TOP = 6
SPAN = 1024
LANES = 128
REQ = ("x", "core")
FLAT = ("x", "core", "exp")
F32 = jnp.float32
BF16 = jnp.bfloat16
MIB = 1 << 20

theta_base = 50000.0
route_scale = 2.446
norm_eps = 1e-06


def rms_scale(values, gain_values):
    widened = values.astype(F32)
    mean_square = jnp.mean(widened * widened, axis=-1, keepdims=True)
    return widened * lax.rsqrt(mean_square + norm_eps) * gain_values.astype(F32)


def rope_angles(positions, rope_width):
    exponent = jnp.arange(rope_width // 2, dtype=F32) * (2.0 / rope_width)
    frequency = jnp.exp(-exponent * math.log(theta_base))
    return positions.astype(F32)[:, None] * frequency[None, :]


def rotate(values, cosine, sine):
    half = values.shape[-1] // 2
    first, second = values[..., :half], values[..., half:]
    return jnp.concatenate(
        [first * cosine - second * sine, second * cosine + first * sine], axis=-1
    )


def dot(a, b):
    return jnp.dot(a, b, preferred_element_type=F32)


def dot_t(a, b):
    return lax.dot_general(a, b, (((1,), (1,)), ((), ())), preferred_element_type=F32)


def whole(shape):
    return pl.BlockSpec(shape, lambda *_: (0,) * len(shape))


def pack_kernel(table, rows_ref, out_ref, padded, made, sems):
    experts, _, cap = made.shape[:3]
    count = rows_ref.shape[0]
    parts = sems.shape[0]
    step = experts // parts
    padded[0:count] = rows_ref[...]
    padded[count] = jnp.zeros(padded.shape[1:], padded.dtype)

    def part_copy(p):
        piece = pl.ds(p * step, step)
        return pltpu.make_async_copy(made.at[piece], out_ref.at[piece], sems.at[p])

    for p in range(parts):

        def one(e, carry):
            for c in range(cap):
                row = padded[table[e * cap + c]]
                made[e, 0, c] = row
                made[e, 1, c] = row
            return carry

        lax.fori_loop(p * step, (p + 1) * step, one, 0)
        part_copy(p).start()
    for p in range(parts):
        part_copy(p).wait()


def pack_rows(table, rows, experts, cap):
    count, blocks, lanes = rows.shape
    shape = (experts, 2, cap, blocks, lanes)
    return pl.pallas_call(
        pack_kernel,
        in_specs=[
            pl.BlockSpec(memory_space=pltpu.SMEM),
            pl.BlockSpec(memory_space=pltpu.VMEM),
        ],
        out_specs=pl.BlockSpec(memory_space=pl.ANY),
        scratch_shapes=[
            pltpu.VMEM((count + 1, blocks, lanes), rows.dtype),
            pltpu.VMEM(shape, rows.dtype),
            pltpu.SemaphoreType.DMA((8,)),
        ],
        out_shape=jax.ShapeDtypeStruct(shape, rows.dtype),
        compiler_params=pltpu.CompilerParams(vmem_limit_bytes=60 * MIB),
    )(table, rows)


def combine_kernel(slots, gates, half_ref, resid_ref, out_ref):
    cap = half_ref.shape[2]

    def one(t, carry):
        total = resid_ref[t].astype(F32)
        mixed = jnp.zeros_like(total)
        for k in range(TOP):
            slot = slots[t * TOP + k]
            expert = slot // cap
            place = slot - expert * cap
            both = half_ref[expert, 0, place].astype(F32) + half_ref[expert, 1, place].astype(F32)
            mixed = mixed + gates[t * TOP + k] * both.astype(BF16).astype(F32)
        out_ref[t] = (total + mixed).astype(BF16)
        return carry

    lax.fori_loop(0, out_ref.shape[0], one, 0, unroll=5)


def combine_rows(slots, gates, halves, resid):
    return pl.pallas_call(
        combine_kernel,
        grid_spec=pltpu.PrefetchScalarGridSpec(
            num_scalar_prefetch=2,
            grid=(1,),
            in_specs=[
                pl.BlockSpec(halves.shape, lambda i, s, g: (0, 0, 0, 0, 0)),
                pl.BlockSpec(resid.shape, lambda i, s, g: (0, 0, 0)),
            ],
            out_specs=pl.BlockSpec(resid.shape, lambda i, s, g: (0, 0, 0)),
        ),
        out_shape=jax.ShapeDtypeStruct(resid.shape, BF16),
        compiler_params=pltpu.CompilerParams(vmem_limit_bytes=32 * MIB),
    )(slots, gates, halves, resid)


def expert_kernel(x_ref, gate_hbm, up_hbm, down_hbm, out_ref, gate_ref, up_ref, down_ref, sems):
    copies = [
        pltpu.make_async_copy(source, target, sems.at[i])
        for i, (source, target) in enumerate(
            ((gate_hbm, gate_ref), (up_hbm, up_ref), (down_hbm, down_ref))
        )
    ]
    opening = pl.program_id(0) == 0

    @pl.when(opening)
    def _():
        for copy in copies:
            copy.start()
        copies[0].wait()
        copies[1].wait()

    rows, blocks, lanes = x_ref.shape
    x = x_ref[...].reshape(rows, blocks * lanes)
    hidden_gate = dot_t(x, gate_ref[0])
    hidden_up = dot_t(x, up_ref[0])
    hidden = (hidden_gate / (1.0 + jnp.exp(-hidden_gate)) * hidden_up).astype(BF16)

    @pl.when(opening)
    def _():
        copies[2].wait()

    step = 4
    for n in range(0, blocks, step):
        part = dot(hidden, down_ref[0, :, n * lanes : (n + step) * lanes]).astype(BF16)
        out_ref[:, n : n + step, :] = part.reshape(rows, step, lanes)


def expert_rows(x, weights):
    rows, blocks, lanes = x.shape
    step = 320
    return pl.pallas_call(
        expert_kernel,
        grid=(rows // step,),
        in_specs=[pl.BlockSpec((step, blocks, lanes), lambda i: (i, 0, 0))]
        + [pl.BlockSpec(memory_space=pl.ANY)] * 3,
        out_specs=pl.BlockSpec((step, blocks, lanes), lambda i: (i, 0, 0)),
        out_shape=jax.ShapeDtypeStruct((rows, blocks, lanes), BF16),
        scratch_shapes=[pltpu.VMEM(w.shape, w.dtype) for w in weights]
        + [pltpu.SemaphoreType.DMA((3,))],
        compiler_params=pltpu.CompilerParams(vmem_limit_bytes=60 * MIB),
        cost_estimate=pl.CostEstimate(
            flops=6 * rows * blocks * lanes * weights[0].shape[1],
            bytes_accessed=4 * rows * blocks * lanes,
            transcendentals=rows * weights[0].shape[1],
        ),
    )(x, *weights)


def project_kernel(
    tokens_ref,
    gain_ref,
    nope_ref,
    rope_ref,
    krope_ref,
    latent_ref,
    latent_gain_ref,
    uk_ref,
    cos_ref,
    sin_ref,
    query_ref,
    key_ref,
    turned,
):
    @pl.when(pl.program_id(0) == 0)
    def _():
        turned[:DR] = rope_ref[...]
        turned[DR:] = krope_ref[...]

    normed = rms_scale(tokens_ref[...], gain_ref[...]).astype(BF16)
    cosine, sine = cos_ref[...], sin_ref[...]

    def turn(v):
        half = DR // 2
        swapped = jnp.concatenate([v[:, half:], v[:, :half]], axis=1)
        return (v * cosine + swapped * sine).astype(BF16)

    ropes = dot_t(normed, turned[...])
    query_ref[:, RANK:] = turn(ropes[:, :DR])
    key_ref[:, RANK:] = turn(ropes[:, DR:])
    nope = dot(normed, nope_ref[...]).astype(BF16)
    query_ref[:, :RANK] = dot_t(nope, uk_ref[...]).astype(BF16)
    latent = dot(normed, latent_ref[...])
    key_ref[:, :RANK] = rms_scale(latent, latent_gain_ref[...]).astype(BF16)


def project(tokens, gain, nope, rope, krope, latent, latent_gain, uk, cosine, sine):
    rows, width = tokens.shape
    step = 208
    fixed = (gain, nope, rope, krope, latent, latent_gain, uk)
    return pl.pallas_call(
        project_kernel,
        grid=(rows // step,),
        in_specs=[pl.BlockSpec((step, width), lambda i: (i, 0))]
        + [
            pl.BlockSpec(a.shape, lambda i: (0, 0), pipeline_mode=pl.Buffered(1))
            for a in fixed
        ]
        + [pl.BlockSpec((step, DR), lambda i: (i, 0))] * 2,
        out_specs=[pl.BlockSpec((step, KEY), lambda i: (i, 0))] * 2,
        out_shape=[jax.ShapeDtypeStruct((rows, KEY), BF16)] * 2,
        scratch_shapes=[pltpu.VMEM((2 * DR, width), BF16)],
        compiler_params=pltpu.CompilerParams(vmem_limit_bytes=32 * MIB),
        cost_estimate=pl.CostEstimate(
            flops=2 * rows * width * (DN + 2 * DR + RANK),
            bytes_accessed=2 * rows * (width + 2 * KEY) + 2 * width * (DN + 2 * DR + RANK),
            transcendentals=0,
        ),
    )(tokens, *fixed, cosine, sine)


def decode_kernel(scale, message_ref, key_ref, seen_ref, out_ref):
    page = message_ref.shape[1] // 9 * 4
    query = message_ref[:, 2 * page, :]
    cache = message_ref[:, page : 2 * page, :].reshape(-1, KEY)
    own = key_ref[...].astype(F32)
    scores = dot_t(query, cache) * scale + seen_ref[...]
    self_score = jnp.sum(query.astype(F32) * own, axis=1, keepdims=True) * scale
    top = jnp.maximum(jnp.max(scores, axis=1, keepdims=True), self_score)
    raised = jnp.exp(scores - top)
    self_raised = jnp.exp(self_score - top)
    total = jnp.sum(raised, axis=1, keepdims=True) + self_raised
    out_ref[...] = (
        dot((raised / total).astype(BF16), cache[:, :RANK])
        + (self_raised / total).astype(BF16).astype(F32) * own[:, :RANK]
    ).astype(BF16)


def decode(message, own_key, seen, scale):
    heads = message.shape[0]
    return pl.pallas_call(
        functools.partial(decode_kernel, scale),
        out_shape=jax.ShapeDtypeStruct((heads, RANK), BF16),
        compiler_params=pltpu.CompilerParams(vmem_limit_bytes=16 * MIB),
        cost_estimate=pl.CostEstimate(
            flops=1 << 25, bytes_accessed=1 << 21, transcendentals=1 << 13
        ),
    )(message, own_key, seen)


def attend_kernel(scale, query_ref, message_ref, new_ref, seen_ref, uv_ref, out_ref):
    step = query_ref.shape[0]
    first = pl.program_id(0) * step
    query = query_ref[...]
    old = message_ref[...].reshape(-1, KEY)
    new = new_ref[...]
    old_scores = dot_t(query, old) * scale + seen_ref[...]
    new_scores = dot_t(query, new) * scale
    rows = lax.broadcasted_iota(jnp.int32, new_scores.shape, 0) + first
    keys = lax.broadcasted_iota(jnp.int32, new_scores.shape, 1)
    new_scores = jnp.where(keys <= rows, new_scores, -jnp.inf)
    top = jnp.maximum(
        jnp.max(old_scores, axis=1, keepdims=True), jnp.max(new_scores, axis=1, keepdims=True)
    )
    old_raised = jnp.exp(old_scores - top)
    new_raised = jnp.exp(new_scores - top)
    total = jnp.sum(old_raised, axis=1, keepdims=True) + jnp.sum(
        new_raised, axis=1, keepdims=True
    )
    share = 1.0 / total
    attended = dot((old_raised * share).astype(BF16), old[:, :RANK]) + dot(
        (new_raised * share).astype(BF16), new[:, :RANK]
    )
    out_ref[...] = dot(attended.astype(BF16), uv_ref[...]).astype(BF16)


def attend(query, message, new, seen, uv, scale):
    step = 256
    pages = message.shape[0]
    page = seen.shape[1] // pages

    def once(shape):
        zeros = (0,) * len(shape)
        return pl.BlockSpec(shape, lambda i: zeros, pipeline_mode=pl.Buffered(1))

    return pl.pallas_call(
        functools.partial(attend_kernel, scale),
        grid=(SPAN // step,),
        in_specs=[
            pl.BlockSpec((step, KEY), lambda i: (i, 0)),
            once((pages, page, KEY)),
            once((SPAN, KEY)),
            once(seen.shape),
            once(uv.shape),
        ],
        out_specs=pl.BlockSpec((step, uv.shape[1]), lambda i: (i, 0)),
        out_shape=jax.ShapeDtypeStruct((SPAN, uv.shape[1]), BF16),
        compiler_params=pltpu.CompilerParams(vmem_limit_bytes=32 * MIB),
        cost_estimate=pl.CostEstimate(
            flops=4 * SPAN * (SPAN + seen.shape[1]) * KEY,
            bytes_accessed=1 << 22,
            transcendentals=SPAN * (SPAN + seen.shape[1]),
        ),
    )(query, message, new, seen, uv)


def after(values):
    return values[(0,) * values.ndim].astype(F32) * 0.0


def seen_bias(page_row, page_size, length):
    pages = page_row.shape[0]
    ids = jnp.arange(pages, dtype=jnp.int32)
    logical = jnp.sum(
        jnp.where(page_row[:, None] == ids[None, :], ids[:, None], 0), axis=0
    )
    inside = jnp.arange(page_size, dtype=jnp.int32)
    position = (logical[:, None] * page_size + inside[None, :]).reshape(1, -1)
    return jnp.where(position < length, 0.0, -jnp.inf).astype(F32)


def shards(
    tokens,
    attn_gain,
    wq_nope,
    wq_rope,
    w_latent,
    w_krope,
    latent_gain,
    w_uk,
    w_uv,
    w_out,
    moe_gain,
    w_router,
    w_gate,
    w_up,
    w_down,
    routes,
    cache_latent,
    cache_rope,
    mig_dest,
    page_table,
    cache_len,
    span_slot,
):
    req_count = lax.axis_size(REQ)
    exp_count = lax.axis_size("exp")
    device_count = req_count * exp_count
    own_exp = lax.axis_index("exp")
    req_group = mig_dest.shape[0]
    move_count = req_group // req_count
    page_size = cache_latent.shape[2]
    rows_group, width = tokens.shape
    rows_device = rows_group // exp_count
    blocks = width // LANES
    scale_factor = 1.0 / math.sqrt(DN + DR)

    half_width = width // 2
    own_core = lax.axis_index("core")
    w_out_half = lax.all_gather(
        lax.dynamic_slice_in_dim(w_out, own_core * half_width, half_width, 1),
        "exp",
        axis=0,
        tiled=True,
    )

    expert_count = w_router.shape[1]
    capacity = 2 * ((rows_device * TOP // expert_count + 5) // 2)
    expert_ids = jnp.arange(expert_count, dtype=jnp.int32)
    named = routes[:, :, None] == expert_ids[None, None, :]
    member = jnp.any(named, axis=1)
    row_ids = jnp.arange(rows_device, dtype=jnp.int32)
    before = (row_ids[None, :] < row_ids[:, None]).astype(BF16)
    rank = dot(before, member.astype(BF16)).astype(jnp.int32)
    slot_of = jnp.sum(
        jnp.where(named, rank[:, None, :] + expert_ids[None, None, :] * capacity, 0), axis=2
    )
    place_ids = jnp.arange(capacity, dtype=jnp.int32)
    filled = member[:, :, None] & (rank[:, :, None] == place_ids[None, None, :])
    table = rows_device + jnp.sum(
        jnp.where(filled, row_ids[:, None, None] - rows_device, 0), axis=0
    )

    slot_ids = jnp.arange(req_group, dtype=jnp.int32)
    earlier = (mig_dest[None, :] == mig_dest[:, None]) & (slot_ids[None, :] < slot_ids[:, None])
    placed = mig_dest * move_count + jnp.sum(earlier.astype(jnp.int32), axis=1)
    order = (placed[None, :] == slot_ids[:, None]).astype(BF16)
    pages = jnp.concatenate(
        [cache_latent[:, 0], cache_rope.reshape(req_group, page_size, DR)], axis=2
    )
    outgoing = jnp.einsum("os,sik->oik", order, pages, preferred_element_type=F32).astype(BF16)
    arrived = lax.all_to_all(
        outgoing.reshape(req_count, move_count * page_size, KEY),
        REQ,
        split_axis=0,
        concat_axis=0,
        tiled=True,
    ).reshape(req_group, page_size, KEY)

    span_len = lax.dynamic_index_in_dim(cache_len, span_slot[0], 0, keepdims=False)
    positions = jnp.concatenate([span_len + jnp.arange(SPAN, dtype=jnp.int32), cache_len])
    angles = rope_angles(positions, DR)
    cosine, sine = jnp.cos(angles), jnp.sin(angles)
    late_cosine, late_sine = cosine[SPAN:], sine[SPAN:]
    late = rms_scale(tokens[SPAN:], attn_gain).astype(BF16)
    late_query = jnp.concatenate(
        [
            dot_t(dot(late, wq_nope).astype(BF16), w_uk).astype(BF16),
            rotate(dot(late, wq_rope), late_cosine, late_sine).astype(BF16),
        ],
        axis=1,
    )

    span_page = lax.dynamic_index_in_dim(arrived, span_slot[0], 0)
    message = jnp.concatenate(
        [
            jnp.broadcast_to(span_page, arrived.shape),
            arrived,
            late_query[:, None, :],
            jnp.zeros((req_group, 7, KEY), BF16),
        ],
        axis=1,
    )
    query, new_keys = project(
        tokens,
        (attn_gain + after(message).astype(BF16))[None, :],
        wq_nope,
        wq_rope.T,
        w_krope.T,
        w_latent,
        latent_gain[None, :],
        w_uk,
        jnp.concatenate([cosine, cosine], axis=1),
        jnp.concatenate([-sine, sine], axis=1),
    )

    message = lax.all_to_all(message, "exp", split_axis=0, concat_axis=0, tiled=True)
    own_len = lax.dynamic_index_in_dim(cache_len, own_exp, 0, keepdims=False)
    own_pages = lax.dynamic_index_in_dim(page_table, own_exp, 0, keepdims=False)
    own_key = lax.dynamic_slice_in_dim(new_keys, SPAN + own_exp, 1, 0)
    own_out = decode(
        message, own_key, seen_bias(own_pages, page_size, own_len), scale_factor
    )
    decode_out = lax.all_to_all(
        own_out[:, None, :], "exp", split_axis=0, concat_axis=0, tiled=True
    )[:, 0]

    span_table = lax.dynamic_index_in_dim(page_table, span_slot[0], 0, keepdims=False)
    span_out = attend(
        query, message, new_keys, seen_bias(span_table, page_size, span_len), w_uv, scale_factor
    )
    head_out = jnp.concatenate([span_out, dot(decode_out, w_uv).astype(BF16)], axis=0)

    heads_in = lax.all_to_all(
        jnp.broadcast_to(
            head_out.reshape(1, exp_count, rows_device, DN), (2, exp_count, rows_device, DN)
        ).reshape(2 * exp_count, rows_device, DN),
        ("core", "exp"),
        split_axis=0,
        concat_axis=0,
        tiled=True,
    ).reshape(2, exp_count, rows_device, DN)
    chip_heads = jnp.transpose(heads_in, (0, 2, 1, 3)).reshape(2 * rows_device, width)
    chip_half = dot(chip_heads, w_out_half).reshape(2, rows_device, half_width)
    own_half = jnp.where(own_core == 0, chip_half[0], chip_half[1])
    other_half = lax.ppermute(
        jnp.where(own_core == 0, chip_half[1], chip_half[0]), "core", [(0, 1), (1, 0)]
    )
    projected = jnp.concatenate(
        [
            jnp.where(own_core == 0, own_half, other_half),
            jnp.where(own_core == 0, other_half, own_half),
        ],
        axis=1,
    )
    own_tokens = lax.dynamic_slice_in_dim(tokens, own_exp * rows_device, rows_device, 0)
    resid = (own_tokens.astype(F32) + projected).astype(BF16)
    moe_in = rms_scale(resid, moe_gain).astype(BF16)
    scores = jax.nn.sigmoid(dot(moe_in, w_router))
    picked = jnp.sum(jnp.where(named, scores[:, None, :], 0.0), axis=2)
    gate_w = route_scale * picked / jnp.sum(picked, axis=1, keepdims=True)

    def spread(rows):
        return lax.all_to_all(
            rows.reshape(device_count, capacity * blocks, LANES),
            FLAT,
            split_axis=0,
            concat_axis=0,
            tiled=True,
        )

    received = spread(
        pack_rows(
            table.reshape(-1),
            moe_in.reshape(rows_device, blocks, LANES),
            expert_count,
            capacity,
        )
    )
    computed = expert_rows(
        received.reshape(device_count * capacity, blocks, LANES),
        (jnp.swapaxes(w_gate, 1, 2), jnp.swapaxes(w_up, 1, 2), w_down),
    )
    mixed = combine_rows(
        slot_of.reshape(-1),
        gate_w.reshape(-1),
        spread(computed).reshape(expert_count, 2, capacity, blocks, LANES),
        resid.reshape(rows_device, blocks, LANES),
    )
    return mixed.reshape(rows_device, width)


def solution(mesh):
    devices = mesh.devices
    split = jax.sharding.Mesh(
        devices.reshape(devices.shape[0] // 2, 2, devices.shape[1]), FLAT
    )
    in_specs = (
        P(REQ, None),
        P(),
        P(None, "exp"),
        P(None, "exp"),
        P(),
        P(),
        P(),
        P(None, "exp"),
        P(None, "exp"),
        P("exp", None),
        P(),
        P(),
        P(FLAT, None, None),
        P(FLAT, None, None),
        P(FLAT, None, None),
        P(FLAT, None),
        P(REQ, "exp", None, None),
        P(REQ, "exp", None),
        P(REQ),
        P(REQ, None),
        P(REQ),
        P(REQ),
    )
    out_specs = P(FLAT, None)
    return jax.shard_map(
        shards, mesh=split, in_specs=in_specs, out_specs=out_specs, check_vma=False
    )
```

```python
import functools
import math

import jax
import jax.numpy as jnp
from jax import lax
from jax.experimental import pallas as pl
from jax.experimental.pallas import tpu as pltpu
from jax.sharding import PartitionSpec as P

DN = 128
DR = 64
RANK = 512
KEY = RANK + DR
TOP = 6
SPAN = 1024
LANES = 128
REQ = ("x", "core")
FLAT = ("x", "core", "exp")
F32 = jnp.float32
BF16 = jnp.bfloat16
MIB = 1 << 20

theta_base = 50000.0
route_scale = 2.446
norm_eps = 1e-06


def rms_scale(values, gain_values):
    widened = values.astype(F32)
    mean_square = jnp.mean(widened * widened, axis=-1, keepdims=True)
    return widened * lax.rsqrt(mean_square + norm_eps) * gain_values.astype(F32)


def rope_angles(positions, rope_width):
    exponent = jnp.arange(rope_width // 2, dtype=F32) * (2.0 / rope_width)
    frequency = jnp.exp(-exponent * math.log(theta_base))
    return positions.astype(F32)[:, None] * frequency[None, :]


def rotate(values, cosine, sine):
    half = values.shape[-1] // 2
    first, second = values[..., :half], values[..., half:]
    return jnp.concatenate(
        [first * cosine - second * sine, second * cosine + first * sine], axis=-1
    )


def dot(a, b):
    return jnp.dot(a, b, preferred_element_type=F32)


def dot_t(a, b):
    return lax.dot_general(a, b, (((1,), (1,)), ((), ())), preferred_element_type=F32)


def whole(shape):
    return pl.BlockSpec(shape, lambda *_: (0,) * len(shape))


def pack_kernel(table, rows_ref, out_ref, padded, made, sems):
    experts, _, cap = made.shape[:3]
    count = rows_ref.shape[0]
    parts = sems.shape[0]
    step = experts // parts
    padded[0:count] = rows_ref[...]
    padded[count] = jnp.zeros(padded.shape[1:], padded.dtype)

    def part_copy(p):
        piece = pl.ds(p * step, step)
        return pltpu.make_async_copy(made.at[piece], out_ref.at[piece], sems.at[p])

    for p in range(parts):

        def one(e, carry):
            for c in range(cap):
                row = padded[table[e * cap + c]]
                made[e, 0, c] = row
                made[e, 1, c] = row
            return carry

        lax.fori_loop(p * step, (p + 1) * step, one, 0)
        part_copy(p).start()
    for p in range(parts):
        part_copy(p).wait()


def pack_rows(table, rows, experts, cap):
    count, blocks, lanes = rows.shape
    shape = (experts, 2, cap, blocks, lanes)
    return pl.pallas_call(
        pack_kernel,
        in_specs=[
            pl.BlockSpec(memory_space=pltpu.SMEM),
            pl.BlockSpec(memory_space=pltpu.VMEM),
        ],
        out_specs=pl.BlockSpec(memory_space=pl.ANY),
        scratch_shapes=[
            pltpu.VMEM((count + 1, blocks, lanes), rows.dtype),
            pltpu.VMEM(shape, rows.dtype),
            pltpu.SemaphoreType.DMA((8,)),
        ],
        out_shape=jax.ShapeDtypeStruct(shape, rows.dtype),
        compiler_params=pltpu.CompilerParams(vmem_limit_bytes=60 * MIB),
    )(table, rows)


def combine_kernel(cap, slots, gates, half_ref, resid_ref, out_ref):
    def one(t, carry):
        mixed = jnp.zeros(out_ref.shape[1:], F32)
        for k in range(TOP):
            slot = slots[t * TOP + k]
            both = half_ref[slot].astype(F32) + half_ref[slot + cap].astype(F32)
            mixed = mixed + gates[t * TOP + k] * both.astype(BF16).astype(F32)
        out_ref[t] = (resid_ref[t].astype(F32) + mixed).astype(BF16)
        return carry

    lax.fori_loop(0, out_ref.shape[0], one, 0, unroll=5)


def combine_rows(cap, slots, gates, halves, resid):
    return pl.pallas_call(
        functools.partial(combine_kernel, cap),
        in_specs=[pl.BlockSpec(memory_space=pltpu.SMEM)] * 2
        + [pl.BlockSpec(memory_space=pltpu.VMEM)] * 2,
        out_specs=pl.BlockSpec(memory_space=pltpu.VMEM),
        out_shape=jax.ShapeDtypeStruct(resid.shape, BF16),
        compiler_params=pltpu.CompilerParams(vmem_limit_bytes=32 * MIB),
    )(slots, gates, halves, resid)


def order_kernel(dest, latent_ref, rope_ref, out_ref, taken):
    move = out_ref.shape[0] // taken.shape[0]
    for g in range(taken.shape[0]):
        taken[g] = 0
    for i in range(out_ref.shape[0]):
        group = dest[i]
        place = group * move + taken[group]
        taken[group] = taken[group] + 1
        out_ref[place, :, :RANK] = latent_ref[i, 0]
        out_ref[place, :, RANK:] = rope_ref[i]


def order_pages(dest, latent, rope, groups):
    slots, _, page, _ = latent.shape
    return pl.pallas_call(
        order_kernel,
        in_specs=[pl.BlockSpec(memory_space=pltpu.SMEM)]
        + [pl.BlockSpec(memory_space=pltpu.VMEM)] * 2,
        out_specs=pl.BlockSpec(memory_space=pltpu.VMEM),
        out_shape=jax.ShapeDtypeStruct((slots, page, KEY), BF16),
        scratch_shapes=[pltpu.SMEM((groups,), jnp.int32)],
        compiler_params=pltpu.CompilerParams(vmem_limit_bytes=32 * MIB),
    )(dest, latent, rope)


def expert_kernel(x_ref, gate_hbm, up_hbm, down_hbm, out_ref, gate_ref, up_ref, down_ref, sems):
    copies = [
        pltpu.make_async_copy(source, target, sems.at[i])
        for i, (source, target) in enumerate(
            ((gate_hbm, gate_ref), (up_hbm, up_ref), (down_hbm, down_ref))
        )
    ]
    opening = pl.program_id(0) == 0

    @pl.when(opening)
    def _():
        for copy in copies:
            copy.start()
        copies[0].wait()
        copies[1].wait()

    rows, blocks, lanes = x_ref.shape
    x = x_ref[...].reshape(rows, blocks * lanes)
    hidden_gate = dot(x, gate_ref[0])
    hidden_up = dot(x, up_ref[0])
    hidden = (hidden_gate / (1.0 + jnp.exp(-hidden_gate)) * hidden_up).astype(BF16)

    @pl.when(opening)
    def _():
        copies[2].wait()

    step = 4
    for n in range(0, blocks, step):
        part = dot(hidden, down_ref[0, :, n * lanes : (n + step) * lanes]).astype(BF16)
        out_ref[:, n : n + step, :] = part.reshape(rows, step, lanes)


def expert_rows(x, weights):
    rows, blocks, lanes = x.shape
    step = 320
    return pl.pallas_call(
        expert_kernel,
        grid=(rows // step,),
        in_specs=[pl.BlockSpec((step, blocks, lanes), lambda i: (i, 0, 0))]
        + [pl.BlockSpec(memory_space=pl.ANY)] * 3,
        out_specs=pl.BlockSpec((step, blocks, lanes), lambda i: (i, 0, 0)),
        out_shape=jax.ShapeDtypeStruct((rows, blocks, lanes), BF16),
        scratch_shapes=[pltpu.VMEM(w.shape, w.dtype) for w in weights]
        + [pltpu.SemaphoreType.DMA((3,))],
        compiler_params=pltpu.CompilerParams(vmem_limit_bytes=60 * MIB),
        cost_estimate=pl.CostEstimate(
            flops=6 * rows * blocks * lanes * weights[0].shape[2],
            bytes_accessed=4 * rows * blocks * lanes,
            transcendentals=rows * weights[0].shape[2],
        ),
    )(x, *weights)


def project_kernel(
    tokens_ref,
    gain_ref,
    nope_ref,
    rope_ref,
    krope_ref,
    latent_ref,
    latent_gain_ref,
    uk_ref,
    cos_ref,
    sin_ref,
    query_ref,
    key_ref,
    turned,
):
    @pl.when(pl.program_id(0) == 0)
    def _():
        turned[:DR] = rope_ref[...]
        turned[DR:] = krope_ref[...]

    normed = rms_scale(tokens_ref[...], gain_ref[...]).astype(BF16)
    cosine, sine = cos_ref[...], sin_ref[...]

    def turn(v):
        half = DR // 2
        swapped = jnp.concatenate([v[:, half:], v[:, :half]], axis=1)
        return (v * cosine + swapped * sine).astype(BF16)

    ropes = dot_t(normed, turned[...])
    query_ref[:, RANK:] = turn(ropes[:, :DR])
    key_ref[:, RANK:] = turn(ropes[:, DR:])
    nope = dot(normed, nope_ref[...]).astype(BF16)
    query_ref[:, :RANK] = dot_t(nope, uk_ref[...]).astype(BF16)
    latent = dot(normed, latent_ref[...])
    key_ref[:, :RANK] = rms_scale(latent, latent_gain_ref[...]).astype(BF16)


def project(tokens, gain, nope, rope, krope, latent, latent_gain, uk, cosine, sine):
    rows, width = tokens.shape
    step = 208
    fixed = (gain, nope, rope, krope, latent, latent_gain, uk)
    return pl.pallas_call(
        project_kernel,
        grid=(rows // step,),
        in_specs=[pl.BlockSpec((step, width), lambda i: (i, 0))]
        + [
            pl.BlockSpec(a.shape, lambda i: (0, 0), pipeline_mode=pl.Buffered(1))
            for a in fixed
        ]
        + [pl.BlockSpec((step, DR), lambda i: (i, 0))] * 2,
        out_specs=[pl.BlockSpec((step, KEY), lambda i: (i, 0))] * 2,
        out_shape=[jax.ShapeDtypeStruct((rows, KEY), BF16)] * 2,
        scratch_shapes=[pltpu.VMEM((2 * DR, width), BF16)],
        compiler_params=pltpu.CompilerParams(vmem_limit_bytes=32 * MIB),
        cost_estimate=pl.CostEstimate(
            flops=2 * rows * width * (DN + 2 * DR + RANK),
            bytes_accessed=2 * rows * (width + 2 * KEY) + 2 * width * (DN + 2 * DR + RANK),
            transcendentals=0,
        ),
    )(tokens, *fixed, cosine, sine)


def decode_kernel(scale, message_ref, key_ref, seen_ref, out_ref):
    page = message_ref.shape[1] // 9 * 4
    query = message_ref[:, 2 * page, :]
    cache = message_ref[:, page : 2 * page, :].reshape(-1, KEY)
    own = key_ref[...].astype(F32)
    scores = dot_t(query, cache) * scale + seen_ref[...]
    self_score = jnp.sum(query.astype(F32) * own, axis=1, keepdims=True) * scale
    top = jnp.maximum(jnp.max(scores, axis=1, keepdims=True), self_score)
    raised = jnp.exp(scores - top)
    self_raised = jnp.exp(self_score - top)
    total = jnp.sum(raised, axis=1, keepdims=True) + self_raised
    out_ref[...] = (
        dot((raised / total).astype(BF16), cache[:, :RANK])
        + (self_raised / total).astype(BF16).astype(F32) * own[:, :RANK]
    ).astype(BF16)


def decode(message, own_key, seen, scale):
    heads = message.shape[0]
    return pl.pallas_call(
        functools.partial(decode_kernel, scale),
        out_shape=jax.ShapeDtypeStruct((heads, RANK), BF16),
        compiler_params=pltpu.CompilerParams(vmem_limit_bytes=16 * MIB),
        cost_estimate=pl.CostEstimate(
            flops=1 << 25, bytes_accessed=1 << 21, transcendentals=1 << 13
        ),
    )(message, own_key, seen)


def attend_kernel(scale, query_ref, message_ref, new_ref, seen_ref, uv_ref, out_ref):
    step = query_ref.shape[0]
    first = pl.program_id(0) * step
    query = query_ref[...]
    old = message_ref[...].reshape(-1, KEY)
    new = new_ref[...]
    old_scores = dot_t(query, old) * scale + seen_ref[...]
    new_scores = dot_t(query, new) * scale
    rows = lax.broadcasted_iota(jnp.int32, new_scores.shape, 0) + first
    keys = lax.broadcasted_iota(jnp.int32, new_scores.shape, 1)
    new_scores = jnp.where(keys <= rows, new_scores, -jnp.inf)
    top = jnp.maximum(
        jnp.max(old_scores, axis=1, keepdims=True), jnp.max(new_scores, axis=1, keepdims=True)
    )
    old_raised = jnp.exp(old_scores - top)
    new_raised = jnp.exp(new_scores - top)
    total = jnp.sum(old_raised, axis=1, keepdims=True) + jnp.sum(
        new_raised, axis=1, keepdims=True
    )
    share = 1.0 / total
    attended = dot((old_raised * share).astype(BF16), old[:, :RANK]) + dot(
        (new_raised * share).astype(BF16), new[:, :RANK]
    )
    out_ref[...] = dot(attended.astype(BF16), uv_ref[...]).astype(BF16)


def attend(query, message, new, seen, uv, scale):
    step = 256
    pages = message.shape[0]
    page = seen.shape[1] // pages

    def once(shape):
        zeros = (0,) * len(shape)
        return pl.BlockSpec(shape, lambda i: zeros, pipeline_mode=pl.Buffered(1))

    return pl.pallas_call(
        functools.partial(attend_kernel, scale),
        grid=(SPAN // step,),
        in_specs=[
            pl.BlockSpec((step, KEY), lambda i: (i, 0)),
            once((pages, page, KEY)),
            once((SPAN, KEY)),
            once(seen.shape),
            once(uv.shape),
        ],
        out_specs=pl.BlockSpec((step, uv.shape[1]), lambda i: (i, 0)),
        out_shape=jax.ShapeDtypeStruct((SPAN, uv.shape[1]), BF16),
        compiler_params=pltpu.CompilerParams(vmem_limit_bytes=32 * MIB),
        cost_estimate=pl.CostEstimate(
            flops=4 * SPAN * (SPAN + seen.shape[1]) * KEY,
            bytes_accessed=1 << 22,
            transcendentals=SPAN * (SPAN + seen.shape[1]),
        ),
    )(query, message, new, seen, uv)


def after(values):
    return values[(0,) * values.ndim].astype(F32) * 0.0


def seen_bias(page_row, page_size, length):
    pages = page_row.shape[0]
    ids = jnp.arange(pages, dtype=jnp.int32)
    logical = jnp.sum(
        jnp.where(page_row[:, None] == ids[None, :], ids[:, None], 0), axis=0
    )
    inside = jnp.arange(page_size, dtype=jnp.int32)
    position = (logical[:, None] * page_size + inside[None, :]).reshape(1, -1)
    return jnp.where(position < length, 0.0, -jnp.inf).astype(F32)


def shards(
    tokens,
    attn_gain,
    wq_nope,
    wq_rope,
    w_latent,
    w_krope,
    latent_gain,
    w_uk,
    w_uv,
    w_out,
    moe_gain,
    w_router,
    w_gate,
    w_up,
    w_down,
    routes,
    cache_latent,
    cache_rope,
    mig_dest,
    page_table,
    cache_len,
    span_slot,
):
    req_count = lax.axis_size(REQ)
    exp_count = lax.axis_size("exp")
    device_count = req_count * exp_count
    own_exp = lax.axis_index("exp")
    req_group = mig_dest.shape[0]
    move_count = req_group // req_count
    page_size = cache_latent.shape[2]
    rows_group, width = tokens.shape
    rows_device = rows_group // exp_count
    blocks = width // LANES
    scale_factor = 1.0 / math.sqrt(DN + DR)

    half_width = width // 2
    own_core = lax.axis_index("core")
    w_out_half = lax.all_gather(
        lax.dynamic_slice_in_dim(w_out, own_core * half_width, half_width, 1),
        "exp",
        axis=0,
        tiled=True,
    )

    expert_count = w_router.shape[1]
    capacity = 2 * ((rows_device * TOP // expert_count + 5) // 2)
    expert_ids = jnp.arange(expert_count, dtype=jnp.int32)
    named = routes[:, :, None] == expert_ids[None, None, :]
    member = jnp.any(named, axis=1)
    row_ids = jnp.arange(rows_device, dtype=jnp.int32)
    before = (row_ids[None, :] < row_ids[:, None]).astype(BF16)
    rank = dot(before, member.astype(BF16)).astype(jnp.int32)
    slot_of = jnp.sum(
        jnp.where(named, rank[:, None, :] + expert_ids[None, None, :] * (2 * capacity), 0),
        axis=2,
    )
    place_ids = jnp.arange(capacity, dtype=jnp.int32)
    filled = member[:, :, None] & (rank[:, :, None] == place_ids[None, None, :])
    table = rows_device + jnp.sum(
        jnp.where(filled, row_ids[:, None, None] - rows_device, 0), axis=0
    )

    outgoing = order_pages(
        mig_dest, cache_latent, cache_rope.reshape(req_group, page_size, DR), req_count
    )
    arrived = lax.all_to_all(
        outgoing.reshape(req_count, move_count * page_size, KEY),
        REQ,
        split_axis=0,
        concat_axis=0,
        tiled=True,
    ).reshape(req_group, page_size, KEY)

    span_len = lax.dynamic_index_in_dim(cache_len, span_slot[0], 0, keepdims=False)
    late_angles = rope_angles(cache_len, DR)
    late_cosine, late_sine = jnp.cos(late_angles), jnp.sin(late_angles)
    late = rms_scale(tokens[SPAN:], attn_gain).astype(BF16)
    late_query = jnp.concatenate(
        [
            dot_t(dot(late, wq_nope).astype(BF16), w_uk).astype(BF16),
            rotate(dot(late, wq_rope), late_cosine, late_sine).astype(BF16),
        ],
        axis=1,
    )

    span_page = lax.dynamic_index_in_dim(arrived, span_slot[0], 0)
    message = jnp.concatenate(
        [
            jnp.broadcast_to(span_page, arrived.shape),
            arrived,
            late_query[:, None, :],
            jnp.zeros((req_group, 7, KEY), BF16),
        ],
        axis=1,
    )
    positions = jnp.concatenate([span_len + jnp.arange(SPAN, dtype=jnp.int32), cache_len])
    angles = rope_angles(positions, DR) + after(message)
    cosine, sine = jnp.cos(angles), jnp.sin(angles)
    query, new_keys = project(
        tokens,
        attn_gain[None, :],
        wq_nope,
        wq_rope.T,
        w_krope.T,
        w_latent,
        latent_gain[None, :],
        w_uk,
        jnp.concatenate([cosine, cosine], axis=1),
        jnp.concatenate([-sine, sine], axis=1),
    )

    message = lax.all_to_all(message, "exp", split_axis=0, concat_axis=0, tiled=True)
    own_len = lax.dynamic_index_in_dim(cache_len, own_exp, 0, keepdims=False)
    own_pages = lax.dynamic_index_in_dim(page_table, own_exp, 0, keepdims=False)
    own_key = lax.dynamic_slice_in_dim(new_keys, SPAN + own_exp, 1, 0)
    own_out = decode(
        message, own_key, seen_bias(own_pages, page_size, own_len), scale_factor
    )
    decode_out = lax.all_to_all(
        own_out[:, None, :], "exp", split_axis=0, concat_axis=0, tiled=True
    )[:, 0]

    span_table = lax.dynamic_index_in_dim(page_table, span_slot[0], 0, keepdims=False)
    span_out = attend(
        query, message, new_keys, seen_bias(span_table, page_size, span_len), w_uv, scale_factor
    )
    head_out = jnp.concatenate([span_out, dot(decode_out, w_uv).astype(BF16)], axis=0)

    heads_in = lax.all_to_all(
        jnp.broadcast_to(
            head_out.reshape(1, exp_count, rows_device, DN), (2, exp_count, rows_device, DN)
        ).reshape(2 * exp_count, rows_device, DN),
        ("core", "exp"),
        split_axis=0,
        concat_axis=0,
        tiled=True,
    ).reshape(2, exp_count, rows_device, DN)
    chip_heads = jnp.transpose(heads_in, (0, 2, 1, 3)).reshape(2 * rows_device, width)
    chip_half = dot(chip_heads, w_out_half).reshape(2, rows_device, half_width)
    own_half = jnp.where(own_core == 0, chip_half[0], chip_half[1])
    other_half = lax.ppermute(
        jnp.where(own_core == 0, chip_half[1], chip_half[0]), "core", [(0, 1), (1, 0)]
    )
    projected = jnp.concatenate(
        [
            jnp.where(own_core == 0, own_half, other_half),
            jnp.where(own_core == 0, other_half, own_half),
        ],
        axis=1,
    )
    own_tokens = lax.dynamic_slice_in_dim(tokens, own_exp * rows_device, rows_device, 0)
    resid = (own_tokens.astype(F32) + projected).astype(BF16)
    moe_in = rms_scale(resid, moe_gain).astype(BF16)
    scores = jax.nn.sigmoid(dot(moe_in, w_router))
    picked = jnp.sum(jnp.where(named, scores[:, None, :], 0.0), axis=2)
    gate_w = route_scale * picked / jnp.sum(picked, axis=1, keepdims=True)

    def spread(rows):
        return lax.all_to_all(
            rows.reshape(device_count, capacity * blocks, LANES),
            FLAT,
            split_axis=0,
            concat_axis=0,
            tiled=True,
        )

    received = spread(
        pack_rows(
            table.reshape(-1),
            moe_in.reshape(rows_device, blocks, LANES),
            expert_count,
            capacity,
        )
    )
    computed = expert_rows(
        received.reshape(device_count * capacity, blocks, LANES),
        (w_gate, w_up, w_down),
    )
    mixed = combine_rows(
        capacity,
        slot_of.reshape(-1),
        gate_w.reshape(-1),
        spread(computed).reshape(device_count * capacity, blocks, LANES),
        resid.reshape(rows_device, blocks, LANES),
    )
    return mixed.reshape(rows_device, width)


def solution(mesh):
    devices = mesh.devices
    split = jax.sharding.Mesh(
        devices.reshape(devices.shape[0] // 2, 2, devices.shape[1]), FLAT
    )
    in_specs = (
        P(REQ, None),
        P(),
        P(None, "exp"),
        P(None, "exp"),
        P(),
        P(),
        P(),
        P(None, "exp"),
        P(None, "exp"),
        P("exp", None),
        P(),
        P(),
        P(FLAT, None, None),
        P(FLAT, None, None),
        P(FLAT, None, None),
        P(FLAT, None),
        P(REQ, "exp", None, None),
        P(REQ, "exp", None),
        P(REQ),
        P(REQ, None),
        P(REQ),
        P(REQ),
    )
    out_specs = P(FLAT, None)
    return jax.shard_map(
        shards, mesh=split, in_specs=in_specs, out_specs=out_specs, check_vma=False
    )
```

```python
import functools
import math

import jax
import jax.numpy as jnp
from jax import lax
from jax.experimental import pallas as pl
from jax.experimental.pallas import tpu as pltpu
from jax.sharding import PartitionSpec as P

DN = 128
DR = 64
RANK = 512
KEY = RANK + DR
TOP = 6
SPAN = 1024
LANES = 128
REQ = ("x", "core")
FLAT = ("x", "core", "exp")
F32 = jnp.float32
BF16 = jnp.bfloat16
MIB = 1 << 20

theta_base = 50000.0
route_scale = 2.446
norm_eps = 1e-06


def rms_scale(values, gain_values):
    widened = values.astype(F32)
    mean_square = jnp.mean(widened * widened, axis=-1, keepdims=True)
    return widened * lax.rsqrt(mean_square + norm_eps) * gain_values.astype(F32)


def rope_angles(positions, rope_width):
    exponent = jnp.arange(rope_width // 2, dtype=F32) * (2.0 / rope_width)
    frequency = jnp.exp(-exponent * math.log(theta_base))
    return positions.astype(F32)[:, None] * frequency[None, :]


def rotate(values, cosine, sine):
    half = values.shape[-1] // 2
    first, second = values[..., :half], values[..., half:]
    return jnp.concatenate(
        [first * cosine - second * sine, second * cosine + first * sine], axis=-1
    )


def dot(a, b):
    return jnp.dot(a, b, preferred_element_type=F32)


def dot_t(a, b):
    return lax.dot_general(a, b, (((1,), (1,)), ((), ())), preferred_element_type=F32)


def whole(shape):
    return pl.BlockSpec(shape, lambda *_: (0,) * len(shape))


def pack_kernel(table, rows_ref, out_ref, padded, made, sems):
    experts, _, cap = made.shape[:3]
    count = rows_ref.shape[0]
    parts = sems.shape[0]
    step = experts // parts
    padded[0:count] = rows_ref[...]
    padded[count] = jnp.zeros(padded.shape[1:], padded.dtype)

    def part_copy(p):
        piece = pl.ds(p * step, step)
        return pltpu.make_async_copy(made.at[piece], out_ref.at[piece], sems.at[p])

    for p in range(parts):

        def one(e, carry):
            for c in range(cap):
                row = padded[table[e * cap + c]]
                made[e, 0, c] = row
                made[e, 1, c] = row
            return carry

        lax.fori_loop(p * step, (p + 1) * step, one, 0)
        part_copy(p).start()
    for p in range(parts):
        part_copy(p).wait()


def pack_rows(table, rows, experts, cap):
    count, blocks, lanes = rows.shape
    shape = (experts, 2, cap, blocks, lanes)
    return pl.pallas_call(
        pack_kernel,
        in_specs=[
            pl.BlockSpec(memory_space=pltpu.SMEM),
            pl.BlockSpec(memory_space=pltpu.VMEM),
        ],
        out_specs=pl.BlockSpec(memory_space=pl.ANY),
        scratch_shapes=[
            pltpu.VMEM((count + 1, blocks, lanes), rows.dtype),
            pltpu.VMEM(shape, rows.dtype),
            pltpu.SemaphoreType.DMA((8,)),
        ],
        out_shape=jax.ShapeDtypeStruct(shape, rows.dtype),
        compiler_params=pltpu.CompilerParams(vmem_limit_bytes=60 * MIB),
    )(table, rows)


def combine_kernel(cap, slots, gates, half_ref, resid_ref, out_ref):
    def one(t, carry):
        mixed = jnp.zeros(out_ref.shape[1:], F32)
        for k in range(TOP):
            slot = slots[t * TOP + k]
            both = half_ref[slot].astype(F32) + half_ref[slot + cap].astype(F32)
            mixed = mixed + gates[t * TOP + k] * both.astype(BF16).astype(F32)
        out_ref[t] = (resid_ref[t].astype(F32) + mixed).astype(BF16)
        return carry

    lax.fori_loop(0, out_ref.shape[0], one, 0, unroll=5)


def combine_rows(cap, slots, gates, halves, resid):
    return pl.pallas_call(
        functools.partial(combine_kernel, cap),
        in_specs=[pl.BlockSpec(memory_space=pltpu.SMEM)] * 2
        + [pl.BlockSpec(memory_space=pltpu.VMEM)] * 2,
        out_specs=pl.BlockSpec(memory_space=pltpu.VMEM),
        out_shape=jax.ShapeDtypeStruct(resid.shape, BF16),
        compiler_params=pltpu.CompilerParams(vmem_limit_bytes=32 * MIB),
    )(slots, gates, halves, resid)


def order_kernel(dest, latent_ref, rope_ref, out_ref, taken):
    move = out_ref.shape[0] // taken.shape[0]
    for g in range(taken.shape[0]):
        taken[g] = 0
    for i in range(out_ref.shape[0]):
        group = dest[i]
        place = group * move + taken[group]
        taken[group] = taken[group] + 1
        out_ref[place, :, :RANK] = latent_ref[i, 0]
        out_ref[place, :, RANK:] = rope_ref[i]


def order_pages(dest, latent, rope, groups):
    slots, _, page, _ = latent.shape
    return pl.pallas_call(
        order_kernel,
        in_specs=[pl.BlockSpec(memory_space=pltpu.SMEM)]
        + [pl.BlockSpec(memory_space=pltpu.VMEM)] * 2,
        out_specs=pl.BlockSpec(memory_space=pltpu.VMEM),
        out_shape=jax.ShapeDtypeStruct((slots, page, KEY), BF16),
        scratch_shapes=[pltpu.SMEM((groups,), jnp.int32)],
        compiler_params=pltpu.CompilerParams(vmem_limit_bytes=32 * MIB),
    )(dest, latent, rope)


def expert_kernel(x_ref, gate_ref, up_ref, down_ref, out_ref):
    rows, blocks, lanes = x_ref.shape
    x = x_ref[...].reshape(rows, blocks * lanes)
    hidden_gate = dot_t(x, gate_ref[0])
    hidden_up = dot_t(x, up_ref[0])
    hidden = (hidden_gate / (1.0 + jnp.exp(-hidden_gate)) * hidden_up).astype(BF16)
    step = 4
    for n in range(0, blocks, step):
        part = dot(hidden, down_ref[0, :, n * lanes : (n + step) * lanes]).astype(BF16)
        out_ref[:, n : n + step, :] = part.reshape(rows, step, lanes)


def expert_rows(x, weights):
    rows, blocks, lanes = x.shape
    step = 320
    return pl.pallas_call(
        expert_kernel,
        grid=(rows // step,),
        in_specs=[pl.BlockSpec((step, blocks, lanes), lambda i: (i, 0, 0))]
        + [pl.BlockSpec(memory_space=pltpu.VMEM)] * 3,
        out_specs=pl.BlockSpec((step, blocks, lanes), lambda i: (i, 0, 0)),
        out_shape=jax.ShapeDtypeStruct((rows, blocks, lanes), BF16),
        compiler_params=pltpu.CompilerParams(vmem_limit_bytes=52 * MIB),
        cost_estimate=pl.CostEstimate(
            flops=6 * rows * blocks * lanes * weights[0].shape[1],
            bytes_accessed=4 * rows * blocks * lanes,
            transcendentals=rows * weights[0].shape[1],
        ),
    )(x, *weights)


def project_kernel(
    tokens_ref,
    gain_ref,
    nope_ref,
    rope_ref,
    krope_ref,
    latent_ref,
    latent_gain_ref,
    uk_ref,
    cos_ref,
    sin_ref,
    query_ref,
    key_ref,
    turned,
):
    @pl.when(pl.program_id(0) == 0)
    def _():
        turned[:DR] = rope_ref[...]
        turned[DR:] = krope_ref[...]

    normed = rms_scale(tokens_ref[...], gain_ref[...]).astype(BF16)
    cosine, sine = cos_ref[...], sin_ref[...]

    def turn(v):
        half = DR // 2
        swapped = jnp.concatenate([v[:, half:], v[:, :half]], axis=1)
        return (v * cosine + swapped * sine).astype(BF16)

    ropes = dot_t(normed, turned[...])
    query_ref[:, RANK:] = turn(ropes[:, :DR])
    key_ref[:, RANK:] = turn(ropes[:, DR:])
    nope = dot(normed, nope_ref[...]).astype(BF16)
    query_ref[:, :RANK] = dot_t(nope, uk_ref[...]).astype(BF16)
    latent = dot(normed, latent_ref[...])
    key_ref[:, :RANK] = rms_scale(latent, latent_gain_ref[...]).astype(BF16)


def project(tokens, gain, nope, rope, krope, latent, latent_gain, uk, cosine, sine):
    rows, width = tokens.shape
    step = 208
    fixed = (gain, nope, rope, krope, latent, latent_gain, uk)
    return pl.pallas_call(
        project_kernel,
        grid=(rows // step,),
        in_specs=[pl.BlockSpec((step, width), lambda i: (i, 0))]
        + [
            pl.BlockSpec(a.shape, lambda i: (0, 0), pipeline_mode=pl.Buffered(1))
            for a in fixed
        ]
        + [pl.BlockSpec((step, DR), lambda i: (i, 0))] * 2,
        out_specs=[pl.BlockSpec((step, KEY), lambda i: (i, 0))] * 2,
        out_shape=[jax.ShapeDtypeStruct((rows, KEY), BF16)] * 2,
        scratch_shapes=[pltpu.VMEM((2 * DR, width), BF16)],
        compiler_params=pltpu.CompilerParams(vmem_limit_bytes=32 * MIB),
        cost_estimate=pl.CostEstimate(
            flops=2 * rows * width * (DN + 2 * DR + RANK),
            bytes_accessed=2 * rows * (width + 2 * KEY) + 2 * width * (DN + 2 * DR + RANK),
            transcendentals=0,
        ),
    )(tokens, *fixed, cosine, sine)


def decode_kernel(scale, message_ref, key_ref, seen_ref, out_ref):
    page = message_ref.shape[1] // 9 * 4
    query = message_ref[:, 2 * page, :]
    cache = message_ref[:, page : 2 * page, :].reshape(-1, KEY)
    own = key_ref[...].astype(F32)
    scores = dot_t(query, cache) * scale + seen_ref[...]
    self_score = jnp.sum(query.astype(F32) * own, axis=1, keepdims=True) * scale
    top = jnp.maximum(jnp.max(scores, axis=1, keepdims=True), self_score)
    raised = jnp.exp(scores - top)
    self_raised = jnp.exp(self_score - top)
    total = jnp.sum(raised, axis=1, keepdims=True) + self_raised
    attended = dot((raised / total).astype(BF16), cache[:, :RANK]) + (
        self_raised / total
    ).astype(BF16).astype(F32) * own[:, :RANK]
    out_ref[...] = attended.astype(BF16).reshape(out_ref.shape)


def decode(message, own_key, seen, scale):
    heads = message.shape[0]
    return pl.pallas_call(
        functools.partial(decode_kernel, scale),
        out_shape=jax.ShapeDtypeStruct((heads, RANK // LANES, LANES), BF16),
        compiler_params=pltpu.CompilerParams(vmem_limit_bytes=16 * MIB),
        cost_estimate=pl.CostEstimate(
            flops=1 << 25, bytes_accessed=1 << 21, transcendentals=1 << 13
        ),
    )(message, own_key, seen)


def attend_kernel(scale, query_ref, message_ref, new_ref, seen_ref, uv_ref, out_ref):
    step = query_ref.shape[0]
    first = pl.program_id(0) * step
    query = query_ref[...]
    old = message_ref[...].reshape(-1, KEY)
    new = new_ref[...]
    old_scores = dot_t(query, old) * scale + seen_ref[...]
    new_scores = dot_t(query, new) * scale
    rows = lax.broadcasted_iota(jnp.int32, new_scores.shape, 0) + first
    keys = lax.broadcasted_iota(jnp.int32, new_scores.shape, 1)
    new_scores = jnp.where(keys <= rows, new_scores, -jnp.inf)
    top = jnp.maximum(
        jnp.max(old_scores, axis=1, keepdims=True), jnp.max(new_scores, axis=1, keepdims=True)
    )
    old_raised = jnp.exp(old_scores - top)
    new_raised = jnp.exp(new_scores - top)
    total = jnp.sum(old_raised, axis=1, keepdims=True) + jnp.sum(
        new_raised, axis=1, keepdims=True
    )
    share = 1.0 / total
    attended = dot((old_raised * share).astype(BF16), old[:, :RANK]) + dot(
        (new_raised * share).astype(BF16), new[:, :RANK]
    )
    out_ref[...] = dot(attended.astype(BF16), uv_ref[...]).astype(BF16)


def attend(query, message, new, seen, uv, scale):
    step = 256
    pages = message.shape[0]
    page = seen.shape[1] // pages

    def once(shape):
        zeros = (0,) * len(shape)
        return pl.BlockSpec(shape, lambda i: zeros, pipeline_mode=pl.Buffered(1))

    return pl.pallas_call(
        functools.partial(attend_kernel, scale),
        grid=(SPAN // step,),
        in_specs=[
            pl.BlockSpec((step, KEY), lambda i: (i, 0)),
            once((pages, page, KEY)),
            once((SPAN, KEY)),
            once(seen.shape),
            once(uv.shape),
        ],
        out_specs=pl.BlockSpec((step, uv.shape[1]), lambda i: (i, 0)),
        out_shape=jax.ShapeDtypeStruct((SPAN, uv.shape[1]), BF16),
        compiler_params=pltpu.CompilerParams(vmem_limit_bytes=32 * MIB),
        cost_estimate=pl.CostEstimate(
            flops=4 * SPAN * (SPAN + seen.shape[1]) * KEY,
            bytes_accessed=1 << 22,
            transcendentals=SPAN * (SPAN + seen.shape[1]),
        ),
    )(query, message, new, seen, uv)


def after(values):
    return values[(0,) * values.ndim].astype(F32) * 0.0


def seen_bias(page_row, page_size, length):
    pages = page_row.shape[0]
    ids = jnp.arange(pages, dtype=jnp.int32)
    logical = jnp.sum(
        jnp.where(page_row[:, None] == ids[None, :], ids[:, None], 0), axis=0
    )
    inside = jnp.arange(page_size, dtype=jnp.int32)
    position = (logical[:, None] * page_size + inside[None, :]).reshape(1, -1)
    return jnp.where(position < length, 0.0, -jnp.inf).astype(F32)


def shards(
    tokens,
    attn_gain,
    wq_nope,
    wq_rope,
    w_latent,
    w_krope,
    latent_gain,
    w_uk,
    w_uv,
    w_out,
    moe_gain,
    w_router,
    w_gate,
    w_up,
    w_down,
    routes,
    cache_latent,
    cache_rope,
    mig_dest,
    page_table,
    cache_len,
    span_slot,
):
    req_count = lax.axis_size(REQ)
    exp_count = lax.axis_size("exp")
    device_count = req_count * exp_count
    own_exp = lax.axis_index("exp")
    req_group = mig_dest.shape[0]
    move_count = req_group // req_count
    page_size = cache_latent.shape[2]
    rows_group, width = tokens.shape
    rows_device = rows_group // exp_count
    blocks = width // LANES
    scale_factor = 1.0 / math.sqrt(DN + DR)

    half_width = width // 2
    own_core = lax.axis_index("core")
    w_out_half = lax.all_gather(
        lax.dynamic_slice_in_dim(w_out, own_core * half_width, half_width, 1),
        "exp",
        axis=0,
        tiled=True,
    )

    expert_count = w_router.shape[1]
    capacity = 2 * ((rows_device * TOP // expert_count + 5) // 2)
    expert_ids = jnp.arange(expert_count, dtype=jnp.int32)
    named = routes[:, :, None] == expert_ids[None, None, :]
    member = jnp.any(named, axis=1)
    row_ids = jnp.arange(rows_device, dtype=jnp.int32)
    before = (row_ids[None, :] < row_ids[:, None]).astype(BF16)
    rank = dot(before, member.astype(BF16)).astype(jnp.int32)
    slot_of = jnp.sum(
        jnp.where(named, rank[:, None, :] + expert_ids[None, None, :] * (2 * capacity), 0),
        axis=2,
    )
    place_ids = jnp.arange(capacity, dtype=jnp.int32)
    filled = member[:, :, None] & (rank[:, :, None] == place_ids[None, None, :])
    table = rows_device + jnp.sum(
        jnp.where(filled, row_ids[:, None, None] - rows_device, 0), axis=0
    )

    outgoing = order_pages(
        mig_dest, cache_latent, cache_rope.reshape(req_group, page_size, DR), req_count
    )
    arrived = lax.all_to_all(
        outgoing.reshape(req_count, move_count * page_size, KEY),
        REQ,
        split_axis=0,
        concat_axis=0,
        tiled=True,
    ).reshape(req_group, page_size, KEY)

    span_len = lax.dynamic_index_in_dim(cache_len, span_slot[0], 0, keepdims=False)
    late_angles = rope_angles(cache_len, DR)
    late_cosine, late_sine = jnp.cos(late_angles), jnp.sin(late_angles)
    late = rms_scale(tokens[SPAN:], attn_gain).astype(BF16)
    late_query = jnp.concatenate(
        [
            dot_t(dot(late, wq_nope).astype(BF16), w_uk).astype(BF16),
            rotate(dot(late, wq_rope), late_cosine, late_sine).astype(BF16),
        ],
        axis=1,
    )

    span_page = lax.dynamic_index_in_dim(arrived, span_slot[0], 0)
    message = jnp.concatenate(
        [
            jnp.broadcast_to(span_page, arrived.shape),
            arrived,
            late_query[:, None, :],
            jnp.zeros((req_group, 7, KEY), BF16),
        ],
        axis=1,
    )
    positions = jnp.concatenate([span_len + jnp.arange(SPAN, dtype=jnp.int32), cache_len])
    angles = rope_angles(positions, DR) + after(message)
    cosine, sine = jnp.cos(angles), jnp.sin(angles)
    query, new_keys = project(
        tokens,
        attn_gain[None, :],
        wq_nope,
        wq_rope.T,
        w_krope.T,
        w_latent,
        latent_gain[None, :],
        w_uk,
        jnp.concatenate([cosine, cosine], axis=1),
        jnp.concatenate([-sine, sine], axis=1),
    )

    message = lax.all_to_all(message, "exp", split_axis=0, concat_axis=0, tiled=True)
    own_len = lax.dynamic_index_in_dim(cache_len, own_exp, 0, keepdims=False)
    own_pages = lax.dynamic_index_in_dim(page_table, own_exp, 0, keepdims=False)
    own_key = lax.dynamic_slice_in_dim(new_keys, SPAN + own_exp, 1, 0)
    own_out = decode(
        message, own_key, seen_bias(own_pages, page_size, own_len), scale_factor
    )
    decode_out = lax.all_to_all(
        own_out, "exp", split_axis=0, concat_axis=0, tiled=True
    ).reshape(req_group, RANK)

    span_table = lax.dynamic_index_in_dim(page_table, span_slot[0], 0, keepdims=False)
    span_out = attend(
        query, message, new_keys, seen_bias(span_table, page_size, span_len), w_uv, scale_factor
    )
    head_out = jnp.concatenate([span_out, dot(decode_out, w_uv).astype(BF16)], axis=0)

    heads_in = lax.all_to_all(
        jnp.broadcast_to(
            head_out.reshape(1, exp_count, rows_device, DN), (2, exp_count, rows_device, DN)
        ).reshape(2 * exp_count, rows_device, DN),
        ("core", "exp"),
        split_axis=0,
        concat_axis=0,
        tiled=True,
    ).reshape(2, exp_count, rows_device, DN)
    chip_heads = jnp.transpose(heads_in, (0, 2, 1, 3)).reshape(2 * rows_device, width)
    chip_half = dot(chip_heads, w_out_half).reshape(2, rows_device, half_width)
    own_half = jnp.where(own_core == 0, chip_half[0], chip_half[1])
    other_half = lax.ppermute(
        jnp.where(own_core == 0, chip_half[1], chip_half[0]), "core", [(0, 1), (1, 0)]
    )
    projected = jnp.concatenate(
        [
            jnp.where(own_core == 0, own_half, other_half),
            jnp.where(own_core == 0, other_half, own_half),
        ],
        axis=1,
    )
    own_tokens = lax.dynamic_slice_in_dim(tokens, own_exp * rows_device, rows_device, 0)
    resid = (own_tokens.astype(F32) + projected).astype(BF16)
    moe_in = rms_scale(resid, moe_gain).astype(BF16)
    scores = jax.nn.sigmoid(dot(moe_in, w_router))
    picked = jnp.sum(jnp.where(named, scores[:, None, :], 0.0), axis=2)
    gate_w = route_scale * picked / jnp.sum(picked, axis=1, keepdims=True)

    def spread(rows):
        return lax.all_to_all(
            rows.reshape(device_count, capacity * blocks, LANES),
            FLAT,
            split_axis=0,
            concat_axis=0,
            tiled=True,
        )

    late_zero = after(moe_in).astype(BF16)
    received = spread(
        pack_rows(
            table.reshape(-1),
            moe_in.reshape(rows_device, blocks, LANES),
            expert_count,
            capacity,
        )
    )
    computed = expert_rows(
        received.reshape(device_count * capacity, blocks, LANES),
        tuple(w + late_zero for w in (jnp.swapaxes(w_gate, 1, 2), jnp.swapaxes(w_up, 1, 2), w_down)),
    )
    mixed = combine_rows(
        capacity,
        slot_of.reshape(-1),
        gate_w.reshape(-1),
        spread(computed).reshape(device_count * capacity, blocks, LANES),
        resid.reshape(rows_device, blocks, LANES),
    )
    return mixed.reshape(rows_device, width)


def solution(mesh):
    devices = mesh.devices
    split = jax.sharding.Mesh(
        devices.reshape(devices.shape[0] // 2, 2, devices.shape[1]), FLAT
    )
    in_specs = (
        P(REQ, None),
        P(),
        P(None, "exp"),
        P(None, "exp"),
        P(),
        P(),
        P(),
        P(None, "exp"),
        P(None, "exp"),
        P("exp", None),
        P(),
        P(),
        P(FLAT, None, None),
        P(FLAT, None, None),
        P(FLAT, None, None),
        P(FLAT, None),
        P(REQ, "exp", None, None),
        P(REQ, "exp", None),
        P(REQ),
        P(REQ, None),
        P(REQ),
        P(REQ),
    )
    out_specs = P(FLAT, None)
    return jax.shard_map(
        shards, mesh=split, in_specs=in_specs, out_specs=out_specs, check_vma=False
    )
```

```python
import functools
import math

import jax
import jax.numpy as jnp
from jax import lax
from jax.experimental import pallas as pl
from jax.experimental.pallas import tpu as pltpu
from jax.sharding import PartitionSpec as P

DN = 128
DR = 64
RANK = 512
KEY = RANK + DR
TOP = 6
SPAN = 1024
LANES = 128
REQ = ("x", "core")
FLAT = ("x", "core", "exp")
F32 = jnp.float32
BF16 = jnp.bfloat16
MIB = 1 << 20

theta_base = 50000.0
route_scale = 2.446
norm_eps = 1e-06


def rms_scale(values, gain_values):
    widened = values.astype(F32)
    mean_square = jnp.mean(widened * widened, axis=-1, keepdims=True)
    return widened * lax.rsqrt(mean_square + norm_eps) * gain_values.astype(F32)


def rope_angles(positions, rope_width):
    exponent = jnp.arange(rope_width // 2, dtype=F32) * (2.0 / rope_width)
    frequency = jnp.exp(-exponent * math.log(theta_base))
    return positions.astype(F32)[:, None] * frequency[None, :]


def rotate(values, cosine, sine):
    half = values.shape[-1] // 2
    first, second = values[..., :half], values[..., half:]
    return jnp.concatenate(
        [first * cosine - second * sine, second * cosine + first * sine], axis=-1
    )


def dot(a, b):
    return jnp.dot(a, b, preferred_element_type=F32)


def dot_t(a, b):
    return lax.dot_general(a, b, (((1,), (1,)), ((), ())), preferred_element_type=F32)


def whole(shape):
    return pl.BlockSpec(shape, lambda *_: (0,) * len(shape))


def pack_kernel(table, rows_ref, out_ref, padded, made, sems):
    experts, _, cap = made.shape[:3]
    count = rows_ref.shape[0]
    parts = sems.shape[0]
    step = experts // parts
    padded[0:count] = rows_ref[...]
    padded[count] = jnp.zeros(padded.shape[1:], padded.dtype)

    def part_copy(p):
        piece = pl.ds(p * step, step)
        return pltpu.make_async_copy(made.at[piece], out_ref.at[piece], sems.at[p])

    for p in range(parts):

        def one(e, carry):
            for c in range(cap):
                row = padded[table[e * cap + c]]
                made[e, 0, c] = row
                made[e, 1, c] = row
            return carry

        lax.fori_loop(p * step, (p + 1) * step, one, 0)
        part_copy(p).start()
    for p in range(parts):
        part_copy(p).wait()


def pack_rows(table, rows, experts, cap):
    count, blocks, lanes = rows.shape
    shape = (experts, 2, cap, blocks, lanes)
    return pl.pallas_call(
        pack_kernel,
        in_specs=[
            pl.BlockSpec(memory_space=pltpu.SMEM),
            pl.BlockSpec(memory_space=pltpu.VMEM),
        ],
        out_specs=pl.BlockSpec(memory_space=pl.ANY),
        scratch_shapes=[
            pltpu.VMEM((count + 1, blocks, lanes), rows.dtype),
            pltpu.VMEM(shape, rows.dtype),
            pltpu.SemaphoreType.DMA((8,)),
        ],
        out_shape=jax.ShapeDtypeStruct(shape, rows.dtype),
        compiler_params=pltpu.CompilerParams(vmem_limit_bytes=60 * MIB),
    )(table, rows)


def combine_kernel(cap, slots, gates, half_ref, resid_ref, out_ref):
    def one(t, carry):
        mixed = jnp.zeros(out_ref.shape[1:], F32)
        for k in range(TOP):
            slot = slots[t * TOP + k]
            both = half_ref[slot].astype(F32) + half_ref[slot + cap].astype(F32)
            mixed = mixed + gates[t * TOP + k] * both.astype(BF16).astype(F32)
        out_ref[t] = (resid_ref[t].astype(F32) + mixed).astype(BF16)
        return carry

    lax.fori_loop(0, out_ref.shape[0], one, 0, unroll=5)


def combine_rows(cap, slots, gates, halves, resid):
    return pl.pallas_call(
        functools.partial(combine_kernel, cap),
        in_specs=[pl.BlockSpec(memory_space=pltpu.SMEM)] * 2
        + [pl.BlockSpec(memory_space=pltpu.VMEM)] * 2,
        out_specs=pl.BlockSpec(memory_space=pltpu.VMEM),
        out_shape=jax.ShapeDtypeStruct(resid.shape, BF16),
        compiler_params=pltpu.CompilerParams(vmem_limit_bytes=32 * MIB),
    )(slots, gates, halves, resid)


def order_kernel(dest, latent_ref, rope_ref, out_ref, taken):
    move = out_ref.shape[0] // taken.shape[0]
    for g in range(taken.shape[0]):
        taken[g] = 0
    for i in range(out_ref.shape[0]):
        group = dest[i]
        place = group * move + taken[group]
        taken[group] = taken[group] + 1
        out_ref[place, :, :RANK] = latent_ref[i, 0]
        out_ref[place, :, RANK:] = rope_ref[i]


def order_pages(dest, latent, rope, groups):
    slots, _, page, _ = latent.shape
    return pl.pallas_call(
        order_kernel,
        in_specs=[pl.BlockSpec(memory_space=pltpu.SMEM)]
        + [pl.BlockSpec(memory_space=pltpu.VMEM)] * 2,
        out_specs=pl.BlockSpec(memory_space=pltpu.VMEM),
        out_shape=jax.ShapeDtypeStruct((slots, page, KEY), BF16),
        scratch_shapes=[pltpu.SMEM((groups,), jnp.int32)],
        compiler_params=pltpu.CompilerParams(vmem_limit_bytes=32 * MIB),
    )(dest, latent, rope)


def expert_kernel(x_ref, gate_ref, up_ref, down_ref, out_ref):
    rows, blocks, lanes = x_ref.shape
    x = x_ref[...].reshape(rows, blocks * lanes)
    hidden_gate = dot_t(x, gate_ref[0])
    hidden_up = dot_t(x, up_ref[0])
    hidden = (hidden_gate / (1.0 + jnp.exp(-hidden_gate)) * hidden_up).astype(BF16)
    step = 4
    for n in range(0, blocks, step):
        part = dot(hidden, down_ref[0, :, n * lanes : (n + step) * lanes]).astype(BF16)
        out_ref[:, n : n + step, :] = part.reshape(rows, step, lanes)


def expert_rows(x, weights):
    rows, blocks, lanes = x.shape
    step = 320
    return pl.pallas_call(
        expert_kernel,
        grid=(rows // step,),
        in_specs=[pl.BlockSpec((step, blocks, lanes), lambda i: (i, 0, 0))]
        + [pl.BlockSpec(memory_space=pltpu.VMEM)] * 3,
        out_specs=pl.BlockSpec((step, blocks, lanes), lambda i: (i, 0, 0)),
        out_shape=jax.ShapeDtypeStruct((rows, blocks, lanes), BF16),
        compiler_params=pltpu.CompilerParams(vmem_limit_bytes=52 * MIB),
        cost_estimate=pl.CostEstimate(
            flops=6 * rows * blocks * lanes * weights[0].shape[1],
            bytes_accessed=4 * rows * blocks * lanes,
            transcendentals=rows * weights[0].shape[1],
        ),
    )(x, *weights)


def project_kernel(
    tokens_ref,
    gain_ref,
    nope_ref,
    rope_ref,
    krope_ref,
    latent_ref,
    latent_gain_ref,
    uk_ref,
    cos_ref,
    sin_ref,
    query_ref,
    key_ref,
    turned,
):
    @pl.when(pl.program_id(0) == 0)
    def _():
        turned[:DR] = rope_ref[...]
        turned[DR:] = krope_ref[...]

    normed = rms_scale(tokens_ref[...], gain_ref[...]).astype(BF16)
    cosine, sine = cos_ref[...], sin_ref[...]

    def turn(v):
        half = DR // 2
        swapped = jnp.concatenate([v[:, half:], v[:, :half]], axis=1)
        return (v * cosine + swapped * sine).astype(BF16)

    ropes = dot_t(normed, turned[...])
    query_ref[:, RANK:] = turn(ropes[:, :DR])
    key_ref[:, RANK:] = turn(ropes[:, DR:])
    nope = dot(normed, nope_ref[...]).astype(BF16)
    query_ref[:, :RANK] = dot_t(nope, uk_ref[...]).astype(BF16)
    latent = dot(normed, latent_ref[...])
    key_ref[:, :RANK] = rms_scale(latent, latent_gain_ref[...]).astype(BF16)


def project(tokens, gain, nope, rope, krope, latent, latent_gain, uk, cosine, sine):
    rows, width = tokens.shape
    step = 208
    fixed = (gain, nope, rope, krope, latent, latent_gain, uk)
    return pl.pallas_call(
        project_kernel,
        grid=(rows // step,),
        in_specs=[pl.BlockSpec((step, width), lambda i: (i, 0))]
        + [
            pl.BlockSpec(a.shape, lambda i: (0, 0), pipeline_mode=pl.Buffered(1))
            for a in fixed
        ]
        + [pl.BlockSpec((step, DR), lambda i: (i, 0))] * 2,
        out_specs=[pl.BlockSpec((step, KEY), lambda i: (i, 0))] * 2,
        out_shape=[jax.ShapeDtypeStruct((rows, KEY), BF16)] * 2,
        scratch_shapes=[pltpu.VMEM((2 * DR, width), BF16)],
        compiler_params=pltpu.CompilerParams(vmem_limit_bytes=32 * MIB),
        cost_estimate=pl.CostEstimate(
            flops=2 * rows * width * (DN + 2 * DR + RANK),
            bytes_accessed=2 * rows * (width + 2 * KEY) + 2 * width * (DN + 2 * DR + RANK),
            transcendentals=0,
        ),
    )(tokens, *fixed, cosine, sine)


def decode_kernel(scale, message_ref, key_ref, seen_ref, out_ref):
    page = message_ref.shape[1] // 9 * 4
    query = message_ref[:, 2 * page, :]
    cache = message_ref[:, page : 2 * page, :].reshape(-1, KEY)
    own = key_ref[...].astype(F32)
    scores = dot_t(query, cache) * scale + seen_ref[...]
    self_score = jnp.sum(query.astype(F32) * own, axis=1, keepdims=True) * scale
    top = jnp.maximum(jnp.max(scores, axis=1, keepdims=True), self_score)
    raised = jnp.exp(scores - top)
    self_raised = jnp.exp(self_score - top)
    total = jnp.sum(raised, axis=1, keepdims=True) + self_raised
    attended = dot((raised / total).astype(BF16), cache[:, :RANK]) + (
        self_raised / total
    ).astype(BF16).astype(F32) * own[:, :RANK]
    out_ref[...] = attended.astype(BF16).reshape(out_ref.shape)


def decode(message, own_key, seen, scale):
    heads = message.shape[0]
    return pl.pallas_call(
        functools.partial(decode_kernel, scale),
        out_shape=jax.ShapeDtypeStruct((heads, RANK // LANES, LANES), BF16),
        compiler_params=pltpu.CompilerParams(vmem_limit_bytes=16 * MIB),
        cost_estimate=pl.CostEstimate(
            flops=1 << 25, bytes_accessed=1 << 21, transcendentals=1 << 13
        ),
    )(message, own_key, seen)


def attend_kernel(scale, query_ref, message_ref, new_ref, seen_ref, uv_ref, out_ref):
    step = query_ref.shape[0]

    def block(index):
        query = query_ref[...]
        old = message_ref[...].reshape(-1, KEY)
        new = new_ref[: (index + 1) * step]
        old_scores = dot_t(query, old) * scale + seen_ref[...]
        new_scores = dot_t(query, new) * scale
        rows = lax.broadcasted_iota(jnp.int32, new_scores.shape, 0) + index * step
        keys = lax.broadcasted_iota(jnp.int32, new_scores.shape, 1)
        new_scores = jnp.where(keys <= rows, new_scores, -jnp.inf)
        top = jnp.maximum(
            jnp.max(old_scores, axis=1, keepdims=True), jnp.max(new_scores, axis=1, keepdims=True)
        )
        old_raised = jnp.exp(old_scores - top)
        new_raised = jnp.exp(new_scores - top)
        total = jnp.sum(old_raised, axis=1, keepdims=True) + jnp.sum(
            new_raised, axis=1, keepdims=True
        )
        share = 1.0 / total
        attended = dot((old_raised * share).astype(BF16), old[:, :RANK]) + dot(
            (new_raised * share).astype(BF16), new[:, :RANK]
        )
        out_ref[...] = dot(attended.astype(BF16), uv_ref[...]).astype(BF16)

    for index in range(SPAN // step):
        pl.when(pl.program_id(0) == index)(functools.partial(block, index))


def attend(query, message, new, seen, uv, scale):
    step = 256
    pages = message.shape[0]
    page = seen.shape[1] // pages

    def once(shape):
        zeros = (0,) * len(shape)
        return pl.BlockSpec(shape, lambda i: zeros, pipeline_mode=pl.Buffered(1))

    return pl.pallas_call(
        functools.partial(attend_kernel, scale),
        grid=(SPAN // step,),
        in_specs=[
            pl.BlockSpec((step, KEY), lambda i: (i, 0)),
            once((pages, page, KEY)),
            once((SPAN, KEY)),
            once(seen.shape),
            once(uv.shape),
        ],
        out_specs=pl.BlockSpec((step, uv.shape[1]), lambda i: (i, 0)),
        out_shape=jax.ShapeDtypeStruct((SPAN, uv.shape[1]), BF16),
        compiler_params=pltpu.CompilerParams(vmem_limit_bytes=32 * MIB),
        cost_estimate=pl.CostEstimate(
            flops=4 * SPAN * (SPAN + seen.shape[1]) * KEY,
            bytes_accessed=1 << 22,
            transcendentals=SPAN * (SPAN + seen.shape[1]),
        ),
    )(query, message, new, seen, uv)


def after(values):
    return values[(0,) * values.ndim].astype(F32) * 0.0


def seen_bias(page_row, page_size, length):
    pages = page_row.shape[0]
    ids = jnp.arange(pages, dtype=jnp.int32)
    logical = jnp.sum(
        jnp.where(page_row[:, None] == ids[None, :], ids[:, None], 0), axis=0
    )
    inside = jnp.arange(page_size, dtype=jnp.int32)
    position = (logical[:, None] * page_size + inside[None, :]).reshape(1, -1)
    return jnp.where(position < length, 0.0, -jnp.inf).astype(F32)


def shards(
    tokens,
    attn_gain,
    wq_nope,
    wq_rope,
    w_latent,
    w_krope,
    latent_gain,
    w_uk,
    w_uv,
    w_out,
    moe_gain,
    w_router,
    w_gate,
    w_up,
    w_down,
    routes,
    cache_latent,
    cache_rope,
    mig_dest,
    page_table,
    cache_len,
    span_slot,
):
    req_count = lax.axis_size(REQ)
    exp_count = lax.axis_size("exp")
    device_count = req_count * exp_count
    own_exp = lax.axis_index("exp")
    req_group = mig_dest.shape[0]
    move_count = req_group // req_count
    page_size = cache_latent.shape[2]
    rows_group, width = tokens.shape
    rows_device = rows_group // exp_count
    blocks = width // LANES
    scale_factor = 1.0 / math.sqrt(DN + DR)

    half_width = width // 2
    own_core = lax.axis_index("core")
    w_out_half = lax.all_gather(
        lax.dynamic_slice_in_dim(w_out, own_core * half_width, half_width, 1),
        "exp",
        axis=0,
        tiled=True,
    )

    expert_count = w_router.shape[1]
    capacity = 2 * ((rows_device * TOP // expert_count + 5) // 2)
    expert_ids = jnp.arange(expert_count, dtype=jnp.int32)
    named = routes[:, :, None] == expert_ids[None, None, :]
    member = jnp.any(named, axis=1)
    row_ids = jnp.arange(rows_device, dtype=jnp.int32)
    before = (row_ids[None, :] < row_ids[:, None]).astype(BF16)
    rank = dot(before, member.astype(BF16)).astype(jnp.int32)
    slot_of = jnp.sum(
        jnp.where(named, rank[:, None, :] + expert_ids[None, None, :] * (2 * capacity), 0),
        axis=2,
    )
    place_ids = jnp.arange(capacity, dtype=jnp.int32)
    filled = member[:, :, None] & (rank[:, :, None] == place_ids[None, None, :])
    table = rows_device + jnp.sum(
        jnp.where(filled, row_ids[:, None, None] - rows_device, 0), axis=0
    )

    outgoing = order_pages(
        mig_dest, cache_latent, cache_rope.reshape(req_group, page_size, DR), req_count
    )
    arrived = lax.all_to_all(
        outgoing.reshape(req_count, move_count * page_size, KEY),
        REQ,
        split_axis=0,
        concat_axis=0,
        tiled=True,
    ).reshape(req_group, page_size, KEY)

    span_len = lax.dynamic_index_in_dim(cache_len, span_slot[0], 0, keepdims=False)
    late_angles = rope_angles(cache_len, DR)
    late_cosine, late_sine = jnp.cos(late_angles), jnp.sin(late_angles)
    late = rms_scale(tokens[SPAN:], attn_gain).astype(BF16)
    late_query = jnp.concatenate(
        [
            dot_t(dot(late, wq_nope).astype(BF16), w_uk).astype(BF16),
            rotate(dot(late, wq_rope), late_cosine, late_sine).astype(BF16),
        ],
        axis=1,
    )

    span_page = lax.dynamic_index_in_dim(arrived, span_slot[0], 0)
    message = jnp.concatenate(
        [
            jnp.broadcast_to(span_page, arrived.shape),
            arrived,
            late_query[:, None, :],
            jnp.zeros((req_group, 7, KEY), BF16),
        ],
        axis=1,
    )
    positions = jnp.concatenate([span_len + jnp.arange(SPAN, dtype=jnp.int32), cache_len])
    angles = rope_angles(positions, DR) + after(message) + after(table)
    cosine, sine = jnp.cos(angles), jnp.sin(angles)
    query, new_keys = project(
        tokens,
        attn_gain[None, :],
        wq_nope,
        wq_rope.T,
        w_krope.T,
        w_latent,
        latent_gain[None, :],
        w_uk,
        jnp.concatenate([cosine, cosine], axis=1),
        jnp.concatenate([-sine, sine], axis=1),
    )

    message = lax.all_to_all(message, "exp", split_axis=0, concat_axis=0, tiled=True)
    own_len = lax.dynamic_index_in_dim(cache_len, own_exp, 0, keepdims=False)
    own_pages = lax.dynamic_index_in_dim(page_table, own_exp, 0, keepdims=False)
    own_key = lax.dynamic_slice_in_dim(new_keys, SPAN + own_exp, 1, 0)
    own_out = decode(
        message, own_key, seen_bias(own_pages, page_size, own_len), scale_factor
    )
    decode_out = lax.all_to_all(
        own_out, "exp", split_axis=0, concat_axis=0, tiled=True
    ).reshape(req_group, RANK)

    span_table = lax.dynamic_index_in_dim(page_table, span_slot[0], 0, keepdims=False)
    span_out = attend(
        query, message, new_keys, seen_bias(span_table, page_size, span_len), w_uv, scale_factor
    )
    head_out = jnp.concatenate([span_out, dot(decode_out, w_uv).astype(BF16)], axis=0)

    heads_in = lax.all_to_all(
        jnp.broadcast_to(
            head_out.reshape(1, exp_count, rows_device, DN), (2, exp_count, rows_device, DN)
        ).reshape(2 * exp_count, rows_device, DN),
        ("core", "exp"),
        split_axis=0,
        concat_axis=0,
        tiled=True,
    ).reshape(2, exp_count, rows_device, DN)
    chip_heads = jnp.transpose(heads_in, (0, 2, 1, 3)).reshape(2 * rows_device, width)
    chip_half = dot(chip_heads, w_out_half).reshape(2, rows_device, half_width)
    own_half = jnp.where(own_core == 0, chip_half[0], chip_half[1])
    other_half = lax.ppermute(
        jnp.where(own_core == 0, chip_half[1], chip_half[0]), "core", [(0, 1), (1, 0)]
    )
    projected = jnp.concatenate(
        [
            jnp.where(own_core == 0, own_half, other_half),
            jnp.where(own_core == 0, other_half, own_half),
        ],
        axis=1,
    )
    own_tokens = lax.dynamic_slice_in_dim(tokens, own_exp * rows_device, rows_device, 0)
    resid = (own_tokens.astype(F32) + projected).astype(BF16)
    moe_in = rms_scale(resid, moe_gain).astype(BF16)
    scores = jax.nn.sigmoid(dot(moe_in, w_router))
    picked = jnp.sum(jnp.where(named, scores[:, None, :], 0.0), axis=2)
    gate_w = route_scale * picked / jnp.sum(picked, axis=1, keepdims=True)

    def spread(rows):
        return lax.all_to_all(
            rows.reshape(device_count, capacity * blocks, LANES),
            FLAT,
            split_axis=0,
            concat_axis=0,
            tiled=True,
        )

    late_zero = after(moe_in).astype(BF16)
    received = spread(
        pack_rows(
            table.reshape(-1),
            moe_in.reshape(rows_device, blocks, LANES),
            expert_count,
            capacity,
        )
    )
    computed = expert_rows(
        received.reshape(device_count * capacity, blocks, LANES),
        tuple(w + late_zero for w in (jnp.swapaxes(w_gate, 1, 2), jnp.swapaxes(w_up, 1, 2), w_down)),
    )
    mixed = combine_rows(
        capacity,
        slot_of.reshape(-1),
        gate_w.reshape(-1),
        spread(computed).reshape(device_count * capacity, blocks, LANES),
        resid.reshape(rows_device, blocks, LANES),
    )
    return mixed.reshape(rows_device, width)


def solution(mesh):
    devices = mesh.devices
    split = jax.sharding.Mesh(
        devices.reshape(devices.shape[0] // 2, 2, devices.shape[1]), FLAT
    )
    in_specs = (
        P(REQ, None),
        P(),
        P(None, "exp"),
        P(None, "exp"),
        P(),
        P(),
        P(),
        P(None, "exp"),
        P(None, "exp"),
        P("exp", None),
        P(),
        P(),
        P(FLAT, None, None),
        P(FLAT, None, None),
        P(FLAT, None, None),
        P(FLAT, None),
        P(REQ, "exp", None, None),
        P(REQ, "exp", None),
        P(REQ),
        P(REQ, None),
        P(REQ),
        P(REQ),
    )
    out_specs = P(FLAT, None)
    return jax.shard_map(
        shards, mesh=split, in_specs=in_specs, out_specs=out_specs, check_vma=False
    )
```
